128 devices in a mesh: visit: 32 (over x, y, core), det: 4 (over z).
Axes of the slice: x: 4, y: 4, z: 4, core: 2. Of those that a mesh axis runs over, the one named last changes fastest.
Arguments:
- images: bfloat16 [8192, 128, 128], P(('visit', 'det'))
- warp_taps: float32 [8192, 2, 8, 128], P(('visit', 'det')), may hold values from -0.3 to 0.7
- warp_shift: int32 [8192, 2], P(('visit', 'det')), may hold values from -3 to 3
- psf_coefs: float32 [8192, 3, 10], P(('visit', 'det')), may hold values from -2.4 to 2.4
- psf_basis: bfloat16 [10, 21, 21], replicated, may hold values from -0.25 to 0.25
- owner: int32 [8192, 1], P(('visit', 'det')), may hold values from 0 to 127; in each aligned block of 64 rows (0 to 63, 64 to 127, ...) at most 2 rows name the same one
- offsets: int32 [8192, 2], P(('visit', 'det')), may hold values from 0 to 3
Outputs:
- difference: float32 [8192, 128, 128], P(('visit', 'det'))
- coadd: float32 [2048, 128, 128], P(('visit', 'det'))
The draws below stay inside these ranges and needn't reach their ends.
Inputs may be any that keep to these rules, and one draw needn't show every extreme that they name: `owner`: among the 64 blocks of one device no patch is named more than 2 times, a bound that some block reaches.
All inputs are finite; a program needn't handle non-finite values.
Results may differ from the reference program's by a relative error of at most 0.0068.
Values may be sent and summed in bfloat16 or wider, within the bound.
No kernel may reach another device: no remote copies, remote signals or barrier semaphores. Data moves between devices by JAX's collectives and lax.ppermute only.
A program may use at most 128 MiB of HBM per device.

```python
import math
import jax
import jax.numpy as jnp
import numpy as np
from jax import lax

S = 128
KER = 21
BASIS = 10
TAPS = 8
PG = 4
NB = 64
CAP = 2
BLOCKS = 8192
TILES = 2048
N_VISIT = 32
N_DET = 4
DEVICES = 128


def draw_images(key, part):
    key = jax.random.fold_in(key, 7)
    first, second = jax.random.split(key)
    noise = jax.random.normal(first, (BLOCKS, S, S), jnp.float32)
    group = (jnp.arange(BLOCKS) // NB % N_DET).astype(jnp.float32)
    ramp = 0.5 * (1.0 + 2.0 * group / max(N_DET - 1, 1))
    jitter = jnp.exp(jax.random.uniform(second, (BLOCKS,), jnp.float32, -0.25, 0.25))
    return (noise * (ramp * jitter)[:, None, None]).astype(jnp.bfloat16)


def set_ends(result, rng, smallest, high):
    place = [jax.random.randint(jax.random.fold_in(rng, axis), (), 0, length) for axis, length in enumerate(result.shape)]
    longest = result.shape.index(max(result.shape))
    neighbour = place[:longest] + [(place[longest] + 1) % result.shape[longest]] + place[longest + 1:]
    return result.at[tuple(place)].set(smallest).at[tuple(neighbour)].set(high)


def level_of(stream_key, shape, shards, low, largest):
    gain = 1.0
    for dim, blocks in shards:
        steps = jax.random.uniform(jax.random.fold_in(jax.random.fold_in(stream_key, 6), dim), (blocks,), jnp.float32, low / len(shards), largest / len(shards))
        gain = gain * jnp.repeat(jnp.exp(steps), shape[dim] // blocks).reshape((-1,) + (1,) * (len(shape) - 1 - dim))
    return gain


def shared_out(own_key, own, number, rows, number_of, top, bound, skew):
    order = jax.random.permutation(own_key, number_of)
    crowded, usual = shares(number_of, rows * top, bound, skew, True), shares(number_of, rows * top, bound, skew, False)
    places = jnp.arange(number_of)

    def named(tallies, turn):
        used = int((tallies > 0).sum())
        fixed = max(1, used // 4)
        shifted = fixed + (places - fixed + turn * (used - fixed)) % max(1, number_of - fixed)
        return jnp.zeros((number_of,), jnp.int32).at[order[jnp.where(places < fixed, places, shifted)]].set(jnp.asarray(tallies, jnp.int32))

    tallies = jnp.where(number % 4 == 0, named(crowded, number // 4), named(usual, number - number // 4 - 1))
    mixed = jax.random.permutation(jax.random.fold_in(own, 3), number_of)
    giver, receiver = mixed[0:number_of // 2 * 2:2], mixed[1:number_of // 2 * 2:2]
    slack = jnp.minimum(tallies[giver] - 1, bound - tallies[receiver]) // 2
    slack = jnp.where((giver == order[0]) | (receiver == order[0]) | (tallies[receiver] == 0), 0, jnp.maximum(slack, 0))
    shifted = jax.random.randint(jax.random.fold_in(own, 4), (number_of // 2,), 0, 1 << 20) % (slack + 1)
    tallies = tallies.at[giver].add(-shifted).at[receiver].add(shifted)
    items = jnp.searchsorted(jnp.cumsum(tallies), jnp.arange(rows * top), side="right").astype(jnp.int32)
    listing = items.reshape(top, rows).T
    listing = listing[jax.random.permutation(jax.random.fold_in(own, 1), rows)]
    turn = jax.random.randint(jax.random.fold_in(own, 2), (rows, 1), 0, top)
    return jnp.take_along_axis(listing, (jnp.arange(top)[None, :] + turn) % top, axis=1)


def shares(count, total, limit, slope, full):
    portions = [(1 << 20) // math.isqrt(standing ** slope) + 1 for standing in range(1, count + 1)]
    largest = limit if full else min(limit, max(-(-total // count), total * portions[0] // sum(portions)))
    least = 1 if total - largest >= count - 1 else 0
    given, rest = [largest] + [least] * (count - 1), total - largest - least * (count - 1)
    while rest > 0:
        candidates = [i for i in range(1, count) if given[i] < largest] or [i for i in range(1, count) if given[i] < limit]
        mass, left = sum([portions[i] for i in candidates]), rest
        for i in candidates:
            addition = min(limit - given[i], max(1, left * portions[i] // mass), rest)
            given[i] = given[i] + addition
            rest = rest - addition
    return np.array(given)


def bell_draw(stream_key, extent, scale, bound, cuts=(), kind=jnp.bfloat16):
    drawn = jax.random.normal(stream_key, extent, jnp.float32) * scale
    if len(cuts) > 0:
        drawn = level_of(stream_key, extent, cuts, -0.22, 0.18) * drawn
    return jnp.clip(drawn, min=-bound, max=bound).astype(kind)


def setup_inputs(seed: int = 0) -> dict:
    streams_of = jax.random.split(jax.random.key(seed), 8)
    images = draw_images(jax.random.fold_in(streams_of[7], 71), 0)
    warp_taps = jnp.clip(-0.3 + 1.0 * jax.random.uniform(streams_of[1], (BLOCKS, 2, TAPS, S), jnp.float32) ** level_of(streams_of[1], (BLOCKS, 2, TAPS, S), ((0, 128),), -0.2, 0.2), -0.3, 0.7)
    warp_shift = set_ends(jax.random.randint(streams_of[2], (BLOCKS, 2), -3, 4), jax.random.fold_in(streams_of[2], 1), -3, 3).astype(jnp.int32)
    psf_coefs = bell_draw(streams_of[3], (BLOCKS, 3, BASIS), 0.4, 2.4, ((0, 128),), jnp.float32)
    psf_basis = bell_draw(streams_of[4], (BASIS, KER, KER), (KER * KER) ** -0.5, 0.25)
    owner_keys = jax.random.split(jax.random.fold_in(streams_of[5], 1), BLOCKS // NB)
    owner_turns = jax.random.permutation(jax.random.fold_in(streams_of[5], 3), BLOCKS // NB)
    owner = jax.vmap(lambda own, number: shared_out(jax.random.fold_in(streams_of[5], 2), own, number, NB, DEVICES, 1, CAP, 2))(owner_keys, owner_turns).reshape((BLOCKS, 1))
    offsets = set_ends(jax.random.randint(streams_of[6], (BLOCKS, 2), 0, PG), jax.random.fold_in(streams_of[6], 1), 0, PG - 1).astype(jnp.int32)
    return {"images": images, "warp_taps": warp_taps, "warp_shift": warp_shift, "psf_coefs": psf_coefs, "psf_basis": psf_basis, "owner": owner, "offsets": offsets}


def build_warp(taps, shift):
    side = taps.shape[-1]
    rows = jnp.arange(side, dtype=jnp.int32)
    total = jnp.zeros((taps.shape[0], side, side), jnp.float32)
    for k in range(taps.shape[1]):
        target = rows[None, :] + shift[:, None] + (k - 3)
        total = total + taps[:, k, :, None] * (rows[None, None, :] == target[:, :, None]).astype(jnp.float32)
    return total.astype(jnp.bfloat16)


def match_blocks(images, taps, shift, coefs, basis):
    west = build_warp(taps[:, 0], shift[:, 0]).astype(jnp.float32)
    east = build_warp(taps[:, 1], shift[:, 1]).astype(jnp.float32)
    half = jnp.einsum('nrc,ncx->nrx', west, images.astype(jnp.float32), precision=lax.Precision.HIGHEST).astype(jnp.bfloat16)
    warped = jnp.einsum('nyc,nxc->nyx', half.astype(jnp.float32), east, precision=lax.Precision.HIGHEST).astype(jnp.bfloat16)
    pad = basis.shape[1] // 2
    response = lax.conv_general_dilated(warped.astype(jnp.float32)[:, None], basis.astype(jnp.float32)[:, None], (1, 1), ((pad, pad), (pad, pad)), dimension_numbers=('NCHW', 'OIHW', 'NCHW'), precision=lax.Precision.HIGHEST)
    side = images.shape[1]
    grid = (2.0 * jnp.arange(side, dtype=jnp.float32) + 1.0 - side) / side
    field = coefs[:, 0, :, None, None] + coefs[:, 1, :, None, None] * grid[None, None, None, :] + coefs[:, 2, :, None, None] * grid[None, None, :, None]
    return jnp.sum(field * response, axis=1)


def reference(images, warp_taps, warp_shift, psf_coefs, psf_basis, owner, offsets):
    def one_device(pieces):
        block_images, taps, shift, coefs = pieces
        matched = match_blocks(block_images, taps, shift, coefs, psf_basis)
        return matched, jnp.sum(matched * matched, axis=(1, 2))

    shaped = (images.reshape(DEVICES, NB, S, S), warp_taps.reshape(DEVICES, NB, 2, TAPS, S), warp_shift.reshape(DEVICES, NB, 2), psf_coefs.reshape(DEVICES, NB, 3, BASIS))
    matched, squares = lax.map(one_device, shaped)
    matched = matched.reshape(BLOCKS, S, S)
    power = jnp.sum(squares.reshape(N_VISIT, N_DET * NB), axis=1)
    weight = (1.0 / (power / (N_DET * NB * S * S) + 1e-6)).astype(jnp.bfloat16).astype(jnp.float32)
    block_weight = jnp.repeat(weight, N_DET * NB)
    sent = matched.astype(jnp.bfloat16).astype(jnp.float32)
    tile = owner[:, 0] * (PG * PG) + offsets[:, 0] * PG + offsets[:, 1]
    numer = jax.ops.segment_sum(block_weight[:, None, None] * sent, tile, TILES)
    denom = jax.ops.segment_sum(block_weight, tile, TILES)
    coadd = numer / jnp.maximum(denom, 0.25)[:, None, None]
    template = coadd.astype(jnp.bfloat16).astype(jnp.float32)[tile]
    return matched - template, coadd
```

```python
import functools

import jax
import jax.numpy as jnp
import numpy as np
from jax import lax
from jax.experimental import pallas as pl
from jax.experimental.pallas import tpu as pltpu
from jax.sharding import PartitionSpec as P

PG = 4
SIDE = 128
TX = 8
TY = 4
WIN = 32
GROUP = 4
ROWS = SIDE // TY
COLS = SIDE // TX


def basis_table(basis):
    kernels, width = basis.shape[0], basis.shape[1]
    w = np.arange(WIN)[:, None] - np.arange(TX)[None, :]
    wide = jnp.pad(basis.astype(jnp.float32), ((0, 0), (0, 0), (0, 1)), constant_values=0.0)
    index = np.where((w >= 0) & (w < width), w, width)
    hot = (index[None] == np.arange(width)[:, None, None]).astype(np.float32)
    table = jnp.einsum("bij,jwt->iwbt", basis.astype(jnp.bfloat16), jnp.asarray(hot, jnp.bfloat16), preferred_element_type=jnp.float32)
    table = table.reshape(width * WIN, kernels * TX).astype(jnp.bfloat16)
    return jnp.concatenate([table, table], axis=1)


def coef_table(coefs):
    count, _, kernels = coefs.shape
    high = lax.reduce_precision(coefs, 8, 7)
    both = jnp.stack([high, coefs - high], axis=1)
    both = jnp.pad(both, ((0, 0), (0, 0), (0, 1), (0, 0)))
    both = jnp.transpose(both, (0, 1, 3, 2))
    both = jnp.repeat(both, TY * TX, axis=3)
    eye = np.tile(np.eye(TX, dtype=np.float32), (1, 4 * TY))
    full = both[:, :, :, None, :] * eye[None, None, None]
    return full.reshape(count, 2 * kernels * TX, 128).astype(jnp.bfloat16)


def pick_table(pad):
    p = np.arange(TY)
    x = np.arange(SIDE)
    X = np.arange(COLS)
    w = np.arange(WIN)
    keep = (w < TX + 2 * pad)[None, None, None, None, :]
    hit = (p[:, None, None, None, None] == p[None, None, None, :, None]) & (
        x[None, :, None, None, None] == TX * X[None, None, :, None, None] + w[None, None, None, None, :] - pad) & keep
    return hit.reshape(TY * SIDE, COLS * TY * WIN)


def grids():
    g = (2.0 * np.arange(SIDE) + 1.0 - SIDE) / SIDE
    lane = np.arange(128)
    h, q, t = lane // 32, (lane // 8) % 4, lane % 8
    gx = np.stack([g[8 * (4 * h + lo) + t] for lo in range(4)])
    gy = g[4 * np.arange(ROWS)[:, None] + q[None, :]]
    return np.concatenate([gy, np.pad(gx, ((0, 4), (0, 0)))]).astype(np.float32)


def kernel(width, shift, images, taps, rtab, ltab, stab, gtab, out, squares, wpad, qf, qb, oscr, zscr):
    step = pl.program_id(0)
    halo = width // 2
    groups = (TY + width - 1) // TY
    rlen = 40
    base = 12

    @pl.when(step == 0)
    def _():
        wpad[...] = jnp.zeros_like(wpad)
        squares[...] = jnp.zeros_like(squares)

    delta = lax.broadcasted_iota(jnp.int32, (SIDE, SIDE), 0) - lax.broadcasted_iota(jnp.int32, (SIDE, SIDE), 1)
    lane = lax.broadcasted_iota(jnp.int32, (8, 128), 1)

    def band(b, d):
        place = delta - (shift[(step * GROUP + b) * 2 + d] - 3)
        total = jnp.zeros((SIDE, SIDE), jnp.float32)
        for k in range(8):
            total = jnp.where(place == k, taps[b, d, k][None, :], total)
        return total.astype(jnp.bfloat16)

    picked = []
    for b in range(GROUP):
        half = lax.dot_general(band(b, 0), images[b], (((0,), (0,)), ((), ())), preferred_element_type=jnp.float32).astype(jnp.bfloat16)
        warped = jnp.dot(half, band(b, 1), preferred_element_type=jnp.float32)
        wpad[b, base:base + SIDE, :] = warped
        phases = [wpad[b, pl.ds(p + base - halo, rlen, stride=TY), :].astype(jnp.bfloat16) for p in range(TY)]
        picked.append(jnp.concatenate(phases, axis=1))
    lhs = jnp.concatenate(picked, axis=0)
    for X in range(COLS):
        got = jnp.dot(lhs, stab[:, 128 * X:128 * X + 128], preferred_element_type=jnp.float32)
        for b in range(GROUP):
            qf[b, pl.ds(X, rlen, stride=COLS), :] = got[b * rlen:(b + 1) * rlen]
    qsub = (lax.broadcasted_iota(jnp.int32, (WIN, 128), 1) // TX) % TY
    group_of = (lane // 32)[:1]
    sub_of = ((lane // 8) % 4)[:1]

    def choose(which, values):
        result = values[3]
        for i in (2, 1, 0):
            result = jnp.where(which == i, values[i], result)
        return result

    ltable = ltab[...]
    for pair in range(0, GROUP, 2):
        rr = jnp.concatenate([rtab[pair], rtab[pair + 1]], axis=1)
        hh = jnp.dot(ltable, rr, preferred_element_type=jnp.float32)
        for b in (pair, pair + 1):
            qb[b] = qf[b].astype(jnp.bfloat16)
            h = hh[:, 128 * (b - pair):128 * (b - pair) + 128]
            zero = jnp.zeros((WIN, 128), jnp.float32)
            parts = []
            for ii in range(width + TY - 1):
                rows = [h[WIN * (ii - q):WIN * (ii - q) + WIN] if 0 <= ii - q < width else zero for q in range(TY)]
                parts.append(choose(qsub, rows).astype(jnp.bfloat16))
            weights = jnp.concatenate(parts, axis=0)
            left = jnp.concatenate([qb[b, COLS * g:COLS * g + ROWS * COLS, :] for g in range(groups)], axis=1)
            oscr[b] = jnp.dot(left, weights, preferred_element_type=jnp.float32)
    for b in range(GROUP):
        mixed = []
        for lo in range(4):
            a = [oscr[b, pl.ds(4 * h + lo, ROWS, stride=COLS), :] for h in range(4)]
            turned = []
            for k in range(4):
                diag = choose(group_of, [a[(g + k) % 4] for g in range(4)])
                turned.append(diag if k == 0 else pltpu.roll(diag, 32 * k, 1))
            m = [choose(group_of, [turned[(h - d) % 4] for h in range(4)]) for d in range(3)]
            mixed.append(m[0] + gtab[ROWS + lo:ROWS + lo + 1, :] * m[1] + gtab[:ROWS, :] * m[2])
        turned = []
        for k in range(4):
            diag = choose(sub_of, [mixed[(g + k) % 4] for g in range(4)])
            if k == 0:
                turned.append(diag)
            else:
                turned.append(jnp.where(sub_of >= k, pltpu.roll(diag, 8 * k, 1), pltpu.roll(diag, (8 * k - 32) % 128, 1)))
        for q in range(4):
            final = choose(sub_of, [turned[(lo - q) % 4] for lo in range(4)])
            zscr[b, pl.ds(q, ROWS, stride=TY), :] = final
            sq = final * final
            squares[...] += sq[0:8] + sq[8:16] + sq[16:24] + sq[24:32]
        out[b] = zscr[b].astype(jnp.bfloat16)


def match(images, warp_taps, warp_shift, psf_coefs, psf_basis):
    count = images.shape[0]
    width = psf_basis.shape[1]
    ltab = basis_table(psf_basis)
    rtab = coef_table(psf_coefs)
    stab = jnp.asarray(pick_table(width // 2), jnp.bfloat16)
    gtab = jnp.asarray(grids())
    whole = lambda a: pl.BlockSpec(a.shape, lambda s, *_: (0,) * a.ndim)
    grid_spec = pltpu.PrefetchScalarGridSpec(
        num_scalar_prefetch=1,
        grid=(count // GROUP,),
        in_specs=[
            pl.BlockSpec((GROUP, SIDE, SIDE), lambda s, *_: (s, 0, 0)),
            pl.BlockSpec((GROUP, 2, 8, SIDE), lambda s, *_: (s, 0, 0, 0)),
            pl.BlockSpec((GROUP,) + rtab.shape[1:], lambda s, *_: (s, 0, 0)),
            whole(ltab), whole(stab), whole(gtab),
        ],
        out_specs=[
            pl.BlockSpec((GROUP, SIDE, SIDE), lambda s, *_: (s, 0, 0)),
            pl.BlockSpec((8, 128), lambda s, *_: (0, 0)),
        ],
        scratch_shapes=[
            pltpu.VMEM((GROUP, 168, SIDE), jnp.float32),
            pltpu.VMEM((GROUP, 640, 128), jnp.float32),
            pltpu.VMEM((GROUP, 640, 128), jnp.bfloat16),
            pltpu.VMEM((GROUP, 512, 128), jnp.float32),
            pltpu.VMEM((GROUP, 128, 128), jnp.float32),
        ],
    )
    return pl.pallas_call(
        functools.partial(kernel, width),
        out_shape=(jax.ShapeDtypeStruct((count, SIDE, SIDE), jnp.bfloat16), jax.ShapeDtypeStruct((8, 128), jnp.float32)),
        grid_spec=grid_spec,
        compiler_params=pltpu.CompilerParams(vmem_limit_bytes=48 * 1024 * 1024),
    )(warp_shift.reshape(-1), images, warp_taps, rtab, ltab, stab, gtab)


def body(images, warp_taps, warp_shift, psf_coefs, psf_basis, owner, offsets):
    count, side = (images.shape[0], images.shape[1])
    sent, squares = match(images, warp_taps, warp_shift, psf_coefs, psf_basis)
    power = lax.psum(jnp.sum(squares), "det")
    entries = count * side * side * lax.axis_size("det")
    weight = (1.0 / (power / entries + 1e-06)).astype(jnp.bfloat16)
    n_visit, n_det = (lax.axis_size("visit"), lax.axis_size("det"))
    devices = n_visit * n_det
    cap = (count + devices - 1) // devices + 1
    slots = devices * cap
    dest = owner[:, 0]
    order = jnp.arange(count, dtype=jnp.int32)
    earlier = (dest[:, None] == dest[None, :]) & (order[:, None] > order[None, :])
    rank = jnp.sum(earlier.astype(jnp.int32), axis=1)
    slot = dest * cap + rank
    tiles = offsets[:, 0] * PG + offsets[:, 1]
    outgoing = (
        jnp.zeros((slots, side, side), jnp.bfloat16).at[slot].set(sent)
    )
    labels = jnp.stack(
        [tiles.astype(jnp.bfloat16), jnp.full((count,), weight, jnp.bfloat16)], axis=1
    )
    outgoing_meta = jnp.zeros((slots, 2), jnp.bfloat16).at[slot].set(labels)
    arrived, arrived_meta = (
        lax.all_to_all(
            outgoing.reshape(devices, cap, side, side),
            ("visit", "det"),
            split_axis=0,
            concat_axis=0,
            tiled=True,
        ),
        lax.all_to_all(
            outgoing_meta.reshape(devices, cap, 2),
            ("visit", "det"),
            split_axis=0,
            concat_axis=0,
            tiled=True,
        ),
    )
    flat = arrived.reshape(slots, side * side)
    flat_meta = arrived_meta.reshape(slots, 2)
    where_tile = flat_meta[:, 0].astype(jnp.float32).astype(jnp.int32)
    positions = PG * PG
    picked = where_tile[None, :] == jnp.arange(positions, dtype=jnp.int32)[:, None]
    scaled = jnp.where(picked, flat_meta[None, :, 1], jnp.zeros((), jnp.bfloat16))
    numer = jnp.dot(scaled, flat, preferred_element_type=jnp.float32)
    denom = jnp.sum(scaled.astype(jnp.float32), axis=1)
    coadd = (numer / jnp.maximum(denom, 0.25)[:, None]).reshape(positions, side, side)
    returning = coadd.astype(jnp.bfloat16)[where_tile]
    templates = lax.all_to_all(
        returning.reshape(devices, cap, side, side),
        ("visit", "det"),
        split_axis=0,
        concat_axis=0,
        tiled=True,
    )
    mine = templates.reshape(slots, side, side)[slot]
    return (sent.astype(jnp.float32) - mine.astype(jnp.float32), coadd)


def solution(mesh):
    in_specs = (
        P(("visit", "det"), None, None),
        P(("visit", "det"), None, None, None),
        P(("visit", "det"), None),
        P(("visit", "det"), None, None),
        P(),
        P(("visit", "det"), None),
        P(("visit", "det"), None),
    )
    out_specs = (P(("visit", "det"), None, None), P(("visit", "det"), None, None))
    return jax.shard_map(body, mesh=mesh, in_specs=in_specs, out_specs=out_specs, check_vma=False)
```

```python
import functools

import jax
import jax.numpy as jnp
import numpy as np
from jax import lax
from jax.experimental import pallas as pl
from jax.experimental.pallas import tpu as pltpu
from jax.sharding import PartitionSpec as P

PG = 4
SIDE = 128
TX = 8
TY = 4
WIN = 32
GROUP = 4
ROWS = SIDE // TY
COLS = SIDE // TX


def basis_table(basis):
    kernels, width = basis.shape[0], basis.shape[1]
    w = np.arange(WIN)[:, None] - np.arange(TX)[None, :]
    wide = jnp.pad(basis.astype(jnp.float32), ((0, 0), (0, 0), (0, 1)), constant_values=0.0)
    index = np.where((w >= 0) & (w < width), w, width)
    hot = (index[None] == np.arange(width)[:, None, None]).astype(np.float32)
    table = jnp.einsum("bij,jwt->iwbt", basis.astype(jnp.bfloat16), jnp.asarray(hot, jnp.bfloat16), preferred_element_type=jnp.float32)
    table = table.reshape(width * WIN, kernels * TX).astype(jnp.bfloat16)
    return jnp.concatenate([table, table], axis=1)


def coef_table(coefs):
    count, _, kernels = coefs.shape
    high = lax.reduce_precision(coefs, 8, 7)
    both = jnp.stack([high, coefs - high], axis=1)
    both = jnp.pad(both, ((0, 0), (0, 0), (0, 1), (0, 0)))
    both = jnp.transpose(both, (0, 1, 3, 2))
    both = jnp.repeat(both, TY * TX, axis=3)
    eye = np.tile(np.eye(TX, dtype=np.float32), (1, 4 * TY))
    full = both[:, :, :, None, :] * eye[None, None, None]
    return full.reshape(count, 2 * kernels * TX, 128).astype(jnp.bfloat16)


def pick_table(pad):
    p = np.arange(TY)
    x = np.arange(SIDE)
    X = np.arange(COLS)
    w = np.arange(WIN)
    keep = (w < TX + 2 * pad)[None, None, None, None, :]
    hit = (p[:, None, None, None, None] == p[None, None, None, :, None]) & (
        x[None, :, None, None, None] == TX * X[None, None, :, None, None] + w[None, None, None, None, :] - pad) & keep
    return hit.reshape(TY * SIDE, COLS * TY * WIN)


def grids():
    g = (2.0 * np.arange(SIDE) + 1.0 - SIDE) / SIDE
    lane = np.arange(128)
    h, q, t = lane // 32, (lane // 8) % 4, lane % 8
    gx = np.stack([g[8 * (4 * h + lo) + t] for lo in range(4)])
    gy = g[4 * np.arange(ROWS)[:, None] + q[None, :]]
    return np.concatenate([gy, np.pad(gx, ((0, 4), (0, 0)))]).astype(np.float32)


def kernel(width, perm, dest, span, shift, *refs):
    images, taps, rtab = refs[:GROUP], refs[GROUP:2 * GROUP], refs[2 * GROUP:3 * GROUP]
    ltab, stab, gtab, before, slots, squares, wpad, qf, qb, oscr, zscr, held, sems = refs[3 * GROUP:]
    step = pl.program_id(0)
    first, last = span[0], span[1]
    turn = lax.rem(step, 2)

    def place(s, b):
        return jnp.minimum(first + s * GROUP + b, perm.shape[0] - 1)

    def live(s, b):
        return first + s * GROUP + b < last

    def copy(s, b):
        spot = lax.rem(s, 2)
        return pltpu.make_async_copy(held.at[spot, b], slots.at[dest[place(s, b)]], sems.at[spot, b])

    def finish(s):
        for b in range(GROUP):
            @pl.when(live(s, b))
            def _():
                copy(s, b).wait()

    halo = width // 2
    groups = (TY + width - 1) // TY
    rlen = 40
    base = 12

    @pl.when(step == 0)
    def _():
        wpad[...] = jnp.zeros_like(wpad)
        squares[...] = before[...]

    @pl.when(first + step * GROUP < last)
    def _():
        delta = lax.broadcasted_iota(jnp.int32, (SIDE, SIDE), 0) - lax.broadcasted_iota(jnp.int32, (SIDE, SIDE), 1)
        lane = lax.broadcasted_iota(jnp.int32, (8, 128), 1)

        def band(b, d):
            off = delta - (shift[perm[place(step, b)] * 2 + d] - 3)
            total = jnp.zeros((SIDE, SIDE), jnp.float32)
            for k in range(8):
                total = jnp.where(off == k, taps[b][0, d, k][None, :], total)
            return total.astype(jnp.bfloat16)

        picked = []
        for b in range(GROUP):
            half = lax.dot_general(band(b, 0), images[b][0], (((0,), (0,)), ((), ())), preferred_element_type=jnp.float32).astype(jnp.bfloat16)
            warped = jnp.dot(half, band(b, 1), preferred_element_type=jnp.float32)
            wpad[b, base:base + SIDE, :] = warped
            phases = [wpad[b, pl.ds(p + base - halo, rlen, stride=TY), :].astype(jnp.bfloat16) for p in range(TY)]
            picked.append(jnp.concatenate(phases, axis=1))
        lhs = jnp.concatenate(picked, axis=0)
        for X in range(COLS):
            got = jnp.dot(lhs, stab[:, 128 * X:128 * X + 128], preferred_element_type=jnp.float32)
            for b in range(GROUP):
                qf[b, pl.ds(X, rlen, stride=COLS), :] = got[b * rlen:(b + 1) * rlen]
        qsub = (lax.broadcasted_iota(jnp.int32, (WIN, 128), 1) // TX) % TY
        group_of = (lane // 32)[:1]
        sub_of = ((lane // 8) % 4)[:1]

        def choose(which, values):
            result = values[3]
            for i in (2, 1, 0):
                result = jnp.where(which == i, values[i], result)
            return result

        ltable = ltab[...]
        for pair in range(0, GROUP, 2):
            rr = jnp.concatenate([rtab[pair][0], rtab[pair + 1][0]], axis=1)
            hh = jnp.dot(ltable, rr, preferred_element_type=jnp.float32)
            for b in (pair, pair + 1):
                qb[b] = qf[b].astype(jnp.bfloat16)
                h = hh[:, 128 * (b - pair):128 * (b - pair) + 128]
                zero = jnp.zeros((WIN, 128), jnp.float32)
                parts = []
                for ii in range(width + TY - 1):
                    rows = [h[WIN * (ii - q):WIN * (ii - q) + WIN] if 0 <= ii - q < width else zero for q in range(TY)]
                    parts.append(choose(qsub, rows).astype(jnp.bfloat16))
                weights = jnp.concatenate(parts, axis=0)
                left = jnp.concatenate([qb[b, COLS * g:COLS * g + ROWS * COLS, :] for g in range(groups)], axis=1)
                oscr[b] = jnp.dot(left, weights, preferred_element_type=jnp.float32)
        @pl.when(step >= 2)
        def _():
            finish(step - 2)

        for b in range(GROUP):
            mixed = []
            for lo in range(4):
                a = [oscr[b, pl.ds(4 * h + lo, ROWS, stride=COLS), :] for h in range(4)]
                turned = []
                for k in range(4):
                    diag = choose(group_of, [a[(g + k) % 4] for g in range(4)])
                    turned.append(diag if k == 0 else pltpu.roll(diag, 32 * k, 1))
                m = [choose(group_of, [turned[(h - d) % 4] for h in range(4)]) for d in range(3)]
                mixed.append(m[0] + gtab[ROWS + lo:ROWS + lo + 1, :] * m[1] + gtab[:ROWS, :] * m[2])
            turned = []
            for k in range(4):
                diag = choose(sub_of, [mixed[(g + k) % 4] for g in range(4)])
                if k == 0:
                    turned.append(diag)
                else:
                    turned.append(jnp.where(sub_of >= k, pltpu.roll(diag, 8 * k, 1), pltpu.roll(diag, (8 * k - 32) % 128, 1)))
            total = jnp.zeros((8, 128), jnp.float32)
            for q in range(4):
                final = choose(sub_of, [turned[(lo - q) % 4] for lo in range(4)])
                zscr[b, pl.ds(q, ROWS, stride=TY), :] = final
                sq = final * final
                total = total + (sq[0:8] + sq[8:16] + sq[16:24] + sq[24:32])
            held[turn, b] = zscr[b].astype(jnp.bfloat16)

            @pl.when(live(step, b))
            def _():
                squares[...] += total
                copy(step, b).start()

        @pl.when(first + (step + 1) * GROUP >= last)
        def _():
            @pl.when(step >= 1)
            def _():
                finish(step - 1)
            finish(step)


def whole(a):
    return pl.BlockSpec(a.shape, lambda s, *_: (0,) * a.ndim)


def match(perm, dest, span, most, tables, images, warp_taps, warp_shift, before, slots):
    rtab, ltab, stab, gtab = tables
    count = images.shape[0]
    width = ltab.shape[0] // WIN

    def one(b, shape):
        def where(s, perm, dest, span, shift):
            return (perm[jnp.minimum(jnp.minimum(span[0] + s * GROUP, jnp.maximum(span[1] - 1, 0)) + b, count - 1)],) + (0,) * (len(shape) - 1)
        return pl.BlockSpec((1,) + shape[1:], where)

    grid_spec = pltpu.PrefetchScalarGridSpec(
        num_scalar_prefetch=4,
        grid=((most + GROUP - 1) // GROUP,),
        in_specs=[one(b, images.shape) for b in range(GROUP)]
        + [one(b, warp_taps.shape) for b in range(GROUP)]
        + [one(b, rtab.shape) for b in range(GROUP)]
        + [whole(ltab), whole(stab), whole(gtab), whole(before)],
        out_specs=[
            pl.BlockSpec(memory_space=pl.ANY),
            pl.BlockSpec((8, 128), lambda s, *_: (0, 0)),
        ],
        scratch_shapes=[
            pltpu.VMEM((GROUP, 168, SIDE), jnp.float32),
            pltpu.VMEM((GROUP, 640, 128), jnp.float32),
            pltpu.VMEM((GROUP, 640, 128), jnp.bfloat16),
            pltpu.VMEM((GROUP, 512, 128), jnp.float32),
            pltpu.VMEM((GROUP, 128, 128), jnp.float32),
            pltpu.VMEM((2, GROUP, 128, 128), jnp.bfloat16),
            pltpu.SemaphoreType.DMA((2, GROUP)),
        ],
    )
    return pl.pallas_call(
        functools.partial(kernel, width),
        out_shape=(jax.ShapeDtypeStruct((slots, SIDE, SIDE), jnp.bfloat16), jax.ShapeDtypeStruct((8, 128), jnp.float32)),
        grid_spec=grid_spec,
        compiler_params=pltpu.CompilerParams(vmem_limit_bytes=48 * 1024 * 1024),
        cost_estimate=pl.CostEstimate(flops=40_000_000_000, bytes_accessed=8_000_000, transcendentals=0),
    )(perm, dest, span, warp_shift.reshape(-1), *[images] * GROUP, *[warp_taps] * GROUP, *[rtab] * GROUP, ltab, stab, gtab, before)


CHUNK = 16


def gather_sum(labels, scale, step, blocks, total):
    for i in range(CHUNK):
        tile = labels[step * CHUNK + i]

        @pl.when(tile >= 0)
        def _():
            total[tile] += scale[step * CHUNK + i] * blocks[i].astype(jnp.float32)


def spread_out(labels, step, templates, out):
    for i in range(CHUNK):
        tile = labels[step * CHUNK + i]

        @pl.when(tile >= 0)
        def _():
            out[i] = templates[tile]


def partial_kernel(labels, scale, blocks, total):
    step = pl.program_id(0)

    @pl.when(step == 0)
    def _():
        total[...] = jnp.zeros_like(total)

    gather_sum(labels, scale, step, blocks, total)


def coadd_kernel(half, labels, scale, inverse, blocks, earlier, coadd, templates, out, total):
    step = pl.program_id(0)

    @pl.when(step == 0)
    def _():
        total[...] = earlier[...]

    @pl.when(step < half)
    def _():
        gather_sum(labels, scale, step, blocks, total)

    @pl.when(step == half - 1)
    def _():
        for tile in range(PG * PG):
            done = total[tile] * inverse[tile]
            coadd[tile] = done
            templates[tile] = done.astype(jnp.bfloat16)

    @pl.when(step >= half)
    def _():
        spread_out(labels, step - half, templates, out)


def spread_kernel(labels, templates, out):
    spread_out(labels, pl.program_id(0), templates, out)


def slots_spec(where):
    return pl.BlockSpec((CHUNK, SIDE, SIDE), lambda s, *_: (where(s), 0, 0))


def partial_sum(labels, scale, blocks):
    tiles = (PG * PG, SIDE, SIDE)
    return pl.pallas_call(
        partial_kernel,
        out_shape=jax.ShapeDtypeStruct(tiles, jnp.float32),
        grid_spec=pltpu.PrefetchScalarGridSpec(
            num_scalar_prefetch=2, grid=(blocks.shape[0] // CHUNK,),
            in_specs=[slots_spec(lambda s: s)],
            out_specs=pl.BlockSpec(tiles, lambda s, *_: (0, 0, 0))),
        cost_estimate=pl.CostEstimate(flops=10_000_000, bytes_accessed=5_000_000, transcendentals=0),
    )(labels, scale, blocks)


def finish_sum(labels, scale, inverse, blocks, earlier):
    tiles = (PG * PG, SIDE, SIDE)
    half = blocks.shape[0] // CHUNK
    full = lambda: pl.BlockSpec(tiles, lambda s, *_: (0, 0, 0))
    return pl.pallas_call(
        functools.partial(coadd_kernel, half),
        out_shape=(jax.ShapeDtypeStruct(tiles, jnp.float32), jax.ShapeDtypeStruct(tiles, jnp.bfloat16), jax.ShapeDtypeStruct(blocks.shape, jnp.bfloat16)),
        grid_spec=pltpu.PrefetchScalarGridSpec(
            num_scalar_prefetch=3, grid=(2 * half,),
            in_specs=[slots_spec(lambda s: jnp.minimum(s, half - 1)), full()],
            out_specs=[full(), full(), slots_spec(lambda s: jnp.maximum(s - half, 0))],
            scratch_shapes=[pltpu.VMEM(tiles, jnp.float32)]),
        compiler_params=pltpu.CompilerParams(vmem_limit_bytes=32 * 1024 * 1024),
        cost_estimate=pl.CostEstimate(flops=10_000_000, bytes_accessed=10_000_000, transcendentals=0),
    )(labels, scale, inverse, blocks, earlier)


def spread(labels, templates, slots):
    return pl.pallas_call(
        spread_kernel,
        out_shape=jax.ShapeDtypeStruct((slots, SIDE, SIDE), jnp.bfloat16),
        grid_spec=pltpu.PrefetchScalarGridSpec(
            num_scalar_prefetch=1, grid=(slots // CHUNK,),
            in_specs=[pl.BlockSpec(templates.shape, lambda s, *_: (0, 0, 0))],
            out_specs=slots_spec(lambda s: s)),
        cost_estimate=pl.CostEstimate(flops=10_000_000, bytes_accessed=5_000_000, transcendentals=0),
    )(labels, templates)


def first_diff_kernel(perm, dest, span, sent, template, out):
    out[...] = sent[...].astype(jnp.float32) - template[...].astype(jnp.float32)


def second_diff_kernel(perm, dest, span, sent, template, held, out):
    live = span[0] < span[1]
    out[...] = jnp.where(live, sent[...].astype(jnp.float32) - template[...].astype(jnp.float32), held[...])


def subtract(perm, dest, span, most, sent, template, held=None):
    count = perm.shape[0]
    at = lambda s, span: jnp.maximum(jnp.minimum(span[0] + s, span[1] - 1), 0)
    one = (1, SIDE, SIDE)
    slot = pl.BlockSpec(one, lambda s, perm, dest, span: (dest[at(s, span)], 0, 0))
    row = pl.BlockSpec(one, lambda s, perm, dest, span: (perm[at(s, span)], 0, 0))
    more = [] if held is None else [held]
    return pl.pallas_call(
        first_diff_kernel if held is None else second_diff_kernel,
        out_shape=jax.ShapeDtypeStruct((count, SIDE, SIDE), jnp.float32),
        grid_spec=pltpu.PrefetchScalarGridSpec(
            num_scalar_prefetch=3, grid=(most,),
            in_specs=[slot, slot] + [row for _ in more],
            out_specs=row),
        input_output_aliases={} if held is None else {5: 0},
        cost_estimate=pl.CostEstimate(flops=10_000_000, bytes_accessed=8_000_000, transcendentals=0),
    )(perm, dest, span, sent, template, *more)


def body(images, warp_taps, warp_shift, psf_coefs, psf_basis, owner, offsets):
    axes = ("visit", "det")
    count = images.shape[0]
    n_visit, n_det = (lax.axis_size("visit"), lax.axis_size("det"))
    devices = n_visit * n_det
    me = lax.axis_index(axes)
    target = owner[:, 0]
    key = target * (PG * PG) + offsets[:, 0] * PG + offsets[:, 1]
    keys = lax.all_gather(key, axes)
    order = jnp.arange(count, dtype=jnp.int32)
    second = jnp.any((target[:, None] == target[None, :]) & (order[:, None] > order[None, :]), axis=1)
    seconds = jnp.sum(second.astype(jnp.int32))
    before_me = order[None, :] < order[:, None]
    lower = jnp.sum((before_me & (second[None, :] == second[:, None])).astype(jnp.int32), axis=1)
    position = jnp.where(second, lower, seconds + lower)
    put = position[None, :] == order[:, None]
    perm = jnp.sum(jnp.where(put, order[None, :], 0), axis=1)
    dest = jnp.sum(jnp.where(put, target[None, :], 0), axis=1)
    zero = jnp.zeros((), jnp.int32)
    span_second = jnp.stack([zero, seconds])
    span_first = jnp.stack([seconds, zero + count])

    tables = (coef_table(psf_coefs), basis_table(psf_basis), jnp.asarray(pick_table(psf_basis.shape[1] // 2), jnp.bfloat16), jnp.asarray(grids()))
    ours = (images, warp_taps, warp_shift)
    exchange = lambda a: lax.all_to_all(a, axes, split_axis=0, concat_axis=0, tiled=True)
    out_second, squares = match(perm, dest, span_second, count // 2, tables, *ours, jnp.zeros((8, 128), jnp.float32), devices)
    in_second = exchange(out_second)
    out_first, squares = match(perm, dest, span_first, count, tables, *ours, squares, devices)
    in_first = exchange(out_first)

    power = lax.all_gather(jnp.sum(squares), axes).reshape(n_visit, n_det).sum(axis=1)
    entries = count * SIDE * SIDE * n_det
    weight = lax.reduce_precision(1.0 / (power / entries + 1e-06), 8, 7)
    scale = jnp.repeat(weight, n_det)
    mine = keys // (PG * PG) == me
    tile = keys % (PG * PG)
    nth = jnp.sum((mine[:, None, :] & (order[None, None, :] < order[None, :, None])).astype(jnp.int32), axis=2)
    label_first = jnp.max(jnp.where(mine & (nth == 0), tile, -1), axis=1)
    label_second = jnp.max(jnp.where(mine & (nth == 1), tile, -1), axis=1)
    kinds = jnp.arange(PG * PG, dtype=jnp.int32)[:, None]
    hits = (label_first[None] == kinds).astype(jnp.float32) + (label_second[None] == kinds).astype(jnp.float32)
    inverse = 1.0 / jnp.maximum(jnp.sum(hits * scale[None], axis=1), 0.25)

    earlier = partial_sum(label_second, scale, in_second)
    coadd, templates, back_first = finish_sum(label_first, scale, inverse, in_first, earlier)
    home_first = exchange(back_first)
    home_second = exchange(spread(label_second, templates, devices))
    difference = subtract(perm, dest, span_first, count, out_first, home_first)
    difference = subtract(perm, dest, span_second, count // 2, out_second, home_second, difference)
    return (difference, coadd)


def solution(mesh):
    in_specs = (
        P(("visit", "det"), None, None),
        P(("visit", "det"), None, None, None),
        P(("visit", "det"), None),
        P(("visit", "det"), None, None),
        P(),
        P(("visit", "det"), None),
        P(("visit", "det"), None),
    )
    out_specs = (P(("visit", "det"), None, None), P(("visit", "det"), None, None))
    return jax.shard_map(body, mesh=mesh, in_specs=in_specs, out_specs=out_specs, check_vma=False)
```

```python
import functools

import jax
import jax.numpy as jnp
import numpy as np
from jax import lax
from jax.experimental import pallas as pl
from jax.experimental.pallas import tpu as pltpu
from jax.sharding import PartitionSpec as P

PG = 4
SIDE = 128
TX = 8
TY = 4
WIN = 32
GROUP = 4
ROWS = SIDE // TY
COLS = SIDE // TX


def basis_table(basis):
    kernels, width = basis.shape[0], basis.shape[1]
    w = np.arange(WIN)[:, None] - np.arange(TX)[None, :]
    wide = jnp.pad(basis.astype(jnp.float32), ((0, 0), (0, 0), (0, 1)), constant_values=0.0)
    index = np.where((w >= 0) & (w < width), w, width)
    hot = (index[None] == np.arange(width)[:, None, None]).astype(np.float32)
    table = jnp.einsum("bij,jwt->iwbt", basis.astype(jnp.bfloat16), jnp.asarray(hot, jnp.bfloat16), preferred_element_type=jnp.float32)
    table = table.reshape(width * WIN, kernels * TX).astype(jnp.bfloat16)
    return jnp.concatenate([table, table], axis=1)


def pick_table(pad):
    p = np.arange(TY)
    x = np.arange(SIDE)
    X = np.arange(COLS)
    w = np.arange(WIN)
    keep = (w < TX + 2 * pad)[None, None, None, None, :]
    hit = (p[:, None, None, None, None] == p[None, None, None, :, None]) & (
        x[None, :, None, None, None] == TX * X[None, None, :, None, None] + w[None, None, None, None, :] - pad) & keep
    return hit.reshape(TY * SIDE, COLS * TY * WIN)


def grids():
    g = (2.0 * np.arange(SIDE) + 1.0 - SIDE) / SIDE
    lane = np.arange(128)
    h, q, t = lane // 32, (lane // 8) % 4, lane % 8
    gx = np.stack([g[8 * (4 * h + lo) + t] for lo in range(4)])
    gy = g[4 * np.arange(ROWS)[:, None] + q[None, :]]
    return np.concatenate([gy, np.pad(gx, ((0, 4), (0, 0)))]).astype(np.float32)


def kernel(width, perm, dest, span, shift, *refs):
    coefs, images, taps, ltab, stab, gtab, before, slots, squares, wpad, qf, qb, oscr, zscr, held, sems = refs
    step = pl.program_id(0)
    first, last = span[0], span[1]
    turn = lax.rem(step, 2)

    def place(s, b):
        return jnp.minimum(first + s * GROUP + b, perm.shape[0] - 1)

    def live(s, b):
        return first + s * GROUP + b < last

    def copy(s, b):
        spot = lax.rem(s, 2)
        return pltpu.make_async_copy(held.at[spot, b], slots.at[dest[place(s, b)]], sems.at[spot, b])

    def finish(s):
        for b in range(GROUP):
            @pl.when(live(s, b))
            def _():
                copy(s, b).wait()

    halo = width // 2
    groups = (TY + width - 1) // TY
    rlen = 40
    base = 12

    @pl.when(step == 0)
    def _():
        wpad[...] = jnp.zeros_like(wpad)
        squares[...] = before[...]

    @pl.when(jnp.logical_and(step >= 2, first + step * GROUP < last))
    def _():
        finish(step - 2)

    chosen = [perm[place(step, b)] for b in range(GROUP)]
    @pl.when(first + step * GROUP < last)
    def _():
        delta = lax.broadcasted_iota(jnp.int32, (SIDE, SIDE), 0) - lax.broadcasted_iota(jnp.int32, (SIDE, SIDE), 1)
        lane = lax.broadcasted_iota(jnp.int32, (8, 128), 1)

        def band(b, d):
            off = delta - (shift[chosen[b] * 2 + d] - 3)
            total = jnp.zeros((SIDE, SIDE), jnp.float32)
            for k in range(8):
                total = jnp.where(off == k, taps[chosen[b], d, k][None, :], total)
            return total.astype(jnp.bfloat16)

        kernels = ltab.shape[1] // (2 * TX)
        lanes = lax.broadcasted_iota(jnp.int32, (TX, 128), 1)
        same = lax.broadcasted_iota(jnp.int32, (TX, 128), 0) == lanes % TX

        def weights_of(b):
            at = chosen[b] * 3 * kernels
            wide = [jnp.where(same, jnp.where(lanes < 32, coefs[at + i], jnp.where(lanes < 64, coefs[at + kernels + i], coefs[at + 2 * kernels + i])), 0.0) for i in range(kernels)]
            wide = jnp.concatenate(wide, axis=0)
            high = wide.astype(jnp.bfloat16)
            low = (wide - high.astype(jnp.float32)).astype(jnp.bfloat16)
            return jnp.concatenate([high, low], axis=0)

        picked = []
        for b in range(GROUP):
            half = lax.dot_general(band(b, 0), images[chosen[b]], (((0,), (0,)), ((), ())), preferred_element_type=jnp.float32).astype(jnp.bfloat16)
            warped = jnp.dot(half, band(b, 1), preferred_element_type=jnp.float32)
            wpad[b, base:base + SIDE, :] = warped
            phases = [wpad[b, pl.ds(p + base - halo, rlen, stride=TY), :].astype(jnp.bfloat16) for p in range(TY)]
            picked.append(jnp.concatenate(phases, axis=1))
        lhs = jnp.concatenate(picked, axis=0)
        for X in range(0, COLS, 2):
            got = jnp.dot(lhs, stab[:, 128 * X:128 * X + 256], preferred_element_type=jnp.float32)
            for b in range(GROUP):
                for side in range(2):
                    qf[b, pl.ds(X + side, rlen, stride=COLS), :] = got[b * rlen:(b + 1) * rlen, 128 * side:128 * side + 128]
        qsub = (lax.broadcasted_iota(jnp.int32, (WIN, 128), 1) // TX) % TY
        group_of = (lane // 32)[:1]
        sub_of = ((lane // 8) % 4)[:1]

        def choose(which, values):
            result = values[3]
            for i in (2, 1, 0):
                result = jnp.where(which == i, values[i], result)
            return result

        ltable = ltab[...]
        for pair in range(0, GROUP, 2):
            rr = jnp.concatenate([weights_of(pair), weights_of(pair + 1)], axis=1)
            hh = jnp.dot(ltable, rr, preferred_element_type=jnp.float32)
            for b in (pair, pair + 1):
                qb[b] = qf[b].astype(jnp.bfloat16)
                h = hh[:, 128 * (b - pair):128 * (b - pair) + 128]
                zero = jnp.zeros((WIN, 128), jnp.float32)
                parts = []
                for ii in range(width + TY - 1):
                    rows = [h[WIN * (ii - q):WIN * (ii - q) + WIN] if 0 <= ii - q < width else zero for q in range(TY)]
                    parts.append(choose(qsub, rows).astype(jnp.bfloat16))
                weights = jnp.concatenate(parts, axis=0)
                left = jnp.concatenate([qb[b, COLS * g:COLS * g + ROWS * COLS, :] for g in range(groups)], axis=1)
                oscr[b] = jnp.dot(left, weights, preferred_element_type=jnp.float32)
        summed = jnp.zeros((8, 128), jnp.float32)
        for b in range(GROUP):
            mixed = []
            for lo in range(4):
                a = [oscr[b, pl.ds(4 * h + lo, ROWS, stride=COLS), :] for h in range(4)]
                turned = []
                for k in range(4):
                    diag = choose(group_of, [a[(g + k) % 4] for g in range(4)])
                    turned.append(diag if k == 0 else pltpu.roll(diag, 32 * k, 1))
                m = [choose(group_of, [turned[(h - d) % 4] for h in range(4)]) for d in range(3)]
                mixed.append(m[0] + gtab[ROWS + lo:ROWS + lo + 1, :] * m[1] + gtab[:ROWS, :] * m[2])
            turned = []
            for k in range(4):
                diag = choose(sub_of, [mixed[(g + k) % 4] for g in range(4)])
                if k == 0:
                    turned.append(diag)
                else:
                    turned.append(jnp.where(sub_of >= k, pltpu.roll(diag, 8 * k, 1), pltpu.roll(diag, (8 * k - 32) % 128, 1)))
            total = jnp.zeros((8, 128), jnp.float32)
            for q in range(4):
                final = choose(sub_of, [turned[(lo - q) % 4] for lo in range(4)])
                zscr[b, pl.ds(q, ROWS, stride=TY), :] = final
                sq = final * final
                total = total + (sq[0:8] + sq[8:16] + sq[16:24] + sq[24:32])
            held[turn, b] = zscr[b].astype(jnp.bfloat16)
            summed = summed + jnp.where(live(step, b), total, 0.0)

        squares[...] += summed
        for b in range(GROUP):
            @pl.when(live(step, b))
            def _():
                copy(step, b).start()

        @pl.when(first + (step + 1) * GROUP >= last)
        def _():
            @pl.when(step >= 1)
            def _():
                finish(step - 1)
            finish(step)


def whole(a):
    return pl.BlockSpec(a.shape, lambda s, *_: (0,) * a.ndim)


def match(perm, dest, span, most, tables, images, warp_taps, shift, coefs, before, slots):
    count = images.shape[0]
    width = tables[0].shape[0] // WIN
    given = (images, warp_taps, *tables, before)
    grid_spec = pltpu.PrefetchScalarGridSpec(
        num_scalar_prefetch=5,
        grid=((most + GROUP - 1) // GROUP,),
        in_specs=[pl.BlockSpec(memory_space=pltpu.VMEM) for _ in given],
        out_specs=[
            pl.BlockSpec(memory_space=pl.ANY),
            pl.BlockSpec((8, 128), lambda s, *_: (0, 0)),
        ],
        scratch_shapes=[
            pltpu.VMEM((GROUP, 168, SIDE), jnp.float32),
            pltpu.VMEM((GROUP, 640, 128), jnp.float32),
            pltpu.VMEM((GROUP, 640, 128), jnp.bfloat16),
            pltpu.VMEM((GROUP, 512, 128), jnp.float32),
            pltpu.VMEM((GROUP, 128, 128), jnp.float32),
            pltpu.VMEM((2, GROUP, 128, 128), jnp.bfloat16),
            pltpu.SemaphoreType.DMA((2, GROUP)),
        ],
    )
    return pl.pallas_call(
        functools.partial(kernel, width),
        out_shape=(jax.ShapeDtypeStruct((slots, SIDE, SIDE), jnp.bfloat16), jax.ShapeDtypeStruct((8, 128), jnp.float32)),
        grid_spec=grid_spec,
        compiler_params=pltpu.CompilerParams(vmem_limit_bytes=56 * 1024 * 1024),
        cost_estimate=pl.CostEstimate(flops=40_000_000_000, bytes_accessed=8_000_000, transcendentals=0),
    )(perm, dest, span, shift, coefs, *given)


CHUNK = 16


def gather_sum(labels, scale, step, blocks, total):
    for i in range(CHUNK):
        tile = labels[step * CHUNK + i]

        @pl.when(tile >= 0)
        def _():
            total[tile] += scale[step * CHUNK + i] * blocks[i].astype(jnp.float32)


def spread_out(labels, step, templates, out):
    for i in range(CHUNK):
        tile = labels[step * CHUNK + i]

        @pl.when(tile >= 0)
        def _():
            out[i] = templates[tile]


def partial_kernel(labels, scale, blocks, total):
    step = pl.program_id(0)

    @pl.when(step == 0)
    def _():
        total[...] = jnp.zeros_like(total)

    gather_sum(labels, scale, step, blocks, total)


def coadd_kernel(half, labels, scale, inverse, blocks, earlier, coadd, templates, out, total):
    step = pl.program_id(0)

    @pl.when(step == 0)
    def _():
        total[...] = earlier[...]

    @pl.when(step < half)
    def _():
        gather_sum(labels, scale, step, blocks, total)

    @pl.when(step == half - 1)
    def _():
        for tile in range(PG * PG):
            done = total[tile] * inverse[tile]
            coadd[tile] = done
            templates[tile] = done.astype(jnp.bfloat16)

    @pl.when(step >= half)
    def _():
        spread_out(labels, step - half, templates, out)


def spread_kernel(labels, templates, out):
    spread_out(labels, pl.program_id(0), templates, out)


def slots_spec(where):
    return pl.BlockSpec((CHUNK, SIDE, SIDE), lambda s, *_: (where(s), 0, 0))


def partial_sum(labels, scale, blocks):
    tiles = (PG * PG, SIDE, SIDE)
    return pl.pallas_call(
        partial_kernel,
        out_shape=jax.ShapeDtypeStruct(tiles, jnp.float32),
        grid_spec=pltpu.PrefetchScalarGridSpec(
            num_scalar_prefetch=2, grid=(blocks.shape[0] // CHUNK,),
            in_specs=[slots_spec(lambda s: s)],
            out_specs=pl.BlockSpec(tiles, lambda s, *_: (0, 0, 0))),
        cost_estimate=pl.CostEstimate(flops=10_000_000, bytes_accessed=5_000_000, transcendentals=0),
    )(labels, scale, blocks)


def finish_sum(labels, scale, inverse, blocks, earlier):
    tiles = (PG * PG, SIDE, SIDE)
    half = blocks.shape[0] // CHUNK
    full = lambda: pl.BlockSpec(tiles, lambda s, *_: (0, 0, 0))
    return pl.pallas_call(
        functools.partial(coadd_kernel, half),
        out_shape=(jax.ShapeDtypeStruct(tiles, jnp.float32), jax.ShapeDtypeStruct(tiles, jnp.bfloat16), jax.ShapeDtypeStruct(blocks.shape, jnp.bfloat16)),
        grid_spec=pltpu.PrefetchScalarGridSpec(
            num_scalar_prefetch=3, grid=(2 * half,),
            in_specs=[slots_spec(lambda s: jnp.minimum(s, half - 1)), full()],
            out_specs=[full(), full(), slots_spec(lambda s: jnp.maximum(s - half, 0))],
            scratch_shapes=[pltpu.VMEM(tiles, jnp.float32)]),
        compiler_params=pltpu.CompilerParams(vmem_limit_bytes=60 * 1024 * 1024),
        cost_estimate=pl.CostEstimate(flops=10_000_000, bytes_accessed=10_000_000, transcendentals=0),
    )(labels, scale, inverse, blocks, earlier)


def spread(labels, templates, slots):
    return pl.pallas_call(
        spread_kernel,
        out_shape=jax.ShapeDtypeStruct((slots, SIDE, SIDE), jnp.bfloat16),
        grid_spec=pltpu.PrefetchScalarGridSpec(
            num_scalar_prefetch=1, grid=(slots // CHUNK,),
            in_specs=[pl.BlockSpec(templates.shape, lambda s, *_: (0, 0, 0))],
            out_specs=slots_spec(lambda s: s)),
        cost_estimate=pl.CostEstimate(flops=10_000_000, bytes_accessed=5_000_000, transcendentals=0),
    )(labels, templates)


def first_diff_kernel(perm, dest, span, sent, template, out):
    out[...] = sent[...].astype(jnp.float32) - template[...].astype(jnp.float32)


def second_diff_kernel(perm, dest, span, sent, template, held, out):
    live = span[0] < span[1]
    out[...] = jnp.where(live, sent[...].astype(jnp.float32) - template[...].astype(jnp.float32), held[...])


def subtract(perm, dest, span, most, sent, template, held=None):
    count = perm.shape[0]
    at = lambda s, span: jnp.maximum(jnp.minimum(span[0] + s, span[1] - 1), 0)
    one = (1, SIDE, SIDE)
    slot = pl.BlockSpec(one, lambda s, perm, dest, span: (dest[at(s, span)], 0, 0))
    row = pl.BlockSpec(one, lambda s, perm, dest, span: (perm[at(s, span)], 0, 0))
    more = [] if held is None else [held]
    return pl.pallas_call(
        first_diff_kernel if held is None else second_diff_kernel,
        out_shape=jax.ShapeDtypeStruct((count, SIDE, SIDE), jnp.float32),
        grid_spec=pltpu.PrefetchScalarGridSpec(
            num_scalar_prefetch=3, grid=(most,),
            in_specs=[slot, slot] + [row for _ in more],
            out_specs=row),
        input_output_aliases={} if held is None else {5: 0},
        cost_estimate=pl.CostEstimate(flops=10_000_000, bytes_accessed=8_000_000, transcendentals=0),
    )(perm, dest, span, sent, template, *more)


def body(images, warp_taps, warp_shift, psf_coefs, psf_basis, owner, offsets):
    axes = ("visit", "det")
    count = images.shape[0]
    n_visit, n_det = (lax.axis_size("visit"), lax.axis_size("det"))
    devices = n_visit * n_det
    target = owner[:, 0]
    tile = offsets[:, 0] * PG + offsets[:, 1]
    order = jnp.arange(count, dtype=jnp.int32)
    second = jnp.any((target[:, None] == target[None, :]) & (order[:, None] > order[None, :]), axis=1)
    seconds = jnp.sum(second.astype(jnp.int32))
    before_me = order[None, :] < order[:, None]
    lower = jnp.sum((before_me & (second[None, :] == second[:, None])).astype(jnp.int32), axis=1)
    position = jnp.where(second, lower, seconds + lower)
    put = position[None, :] == order[:, None]
    perm = jnp.sum(jnp.where(put, order[None, :], 0), axis=1)
    dest = jnp.sum(jnp.where(put, target[None, :], 0), axis=1)
    zero = jnp.zeros((), jnp.int32)
    span_second = jnp.stack([zero, seconds])
    span_first = jnp.stack([seconds, zero + count])

    tables = (basis_table(psf_basis), jnp.asarray(pick_table(psf_basis.shape[1] // 2), jnp.bfloat16), jnp.asarray(grids()))
    ours = (images, warp_taps, warp_shift.reshape(-1), psf_coefs.reshape(-1))
    exchange = lambda a: lax.all_to_all(a, axes, split_axis=0, concat_axis=0, tiled=True)
    out_second, squares = match(perm, dest, span_second, count // 2, tables, *ours, jnp.zeros((8, 128), jnp.float32), devices)
    in_second = exchange(out_second)
    out_first, squares = match(perm, dest, span_first, count, tables, *ours, squares, devices)
    in_second, out_first, squares = lax.optimization_barrier((in_second, out_first, squares))
    named = target[None, :] == jnp.arange(devices, dtype=jnp.int32)[:, None]
    label = lambda rank: jnp.max(jnp.where(named & (second == rank)[None, :], tile[None, :], -1), axis=1).astype(jnp.float32)
    note = jnp.stack([jnp.full((devices,), jnp.sum(squares)), label(False), label(True)], axis=1)
    notes = exchange(note)
    out_first, notes = lax.optimization_barrier((out_first, notes))
    in_first = exchange(out_first)
    power = notes[:, 0].reshape(n_visit, n_det).sum(axis=1)
    entries = count * SIDE * SIDE * n_det
    weight = lax.reduce_precision(1.0 / (power / entries + 1e-06), 8, 7)
    scale = jnp.repeat(weight, n_det)
    label_first, label_second = notes[:, 1].astype(jnp.int32), notes[:, 2].astype(jnp.int32)
    kinds = jnp.arange(PG * PG, dtype=jnp.int32)[:, None]
    hits = (label_first[None] == kinds).astype(jnp.float32) + (label_second[None] == kinds).astype(jnp.float32)
    inverse = 1.0 / jnp.maximum(jnp.sum(hits * scale[None], axis=1), 0.25)

    earlier = partial_sum(label_second, scale, in_second)
    coadd, templates, back_first = finish_sum(label_first, scale, inverse, in_first, earlier)
    home_first = exchange(back_first)
    home_second = exchange(spread(label_second, templates, devices))
    difference = subtract(perm, dest, span_first, count, out_first, home_first)
    difference = subtract(perm, dest, span_second, count // 2, out_second, home_second, difference)
    return (difference, coadd)


def solution(mesh):
    in_specs = (
        P(("visit", "det"), None, None),
        P(("visit", "det"), None, None, None),
        P(("visit", "det"), None),
        P(("visit", "det"), None, None),
        P(),
        P(("visit", "det"), None),
        P(("visit", "det"), None),
    )
    out_specs = (P(("visit", "det"), None, None), P(("visit", "det"), None, None))
    return jax.shard_map(body, mesh=mesh, in_specs=in_specs, out_specs=out_specs, check_vma=False)
```

```python
import functools

import jax
import jax.numpy as jnp
import numpy as np
from jax import lax
from jax.experimental import pallas as pl
from jax.experimental.pallas import tpu as pltpu
from jax.sharding import PartitionSpec as P

PG = 4
SIDE = 128
TX = 8
TY = 4
WIN = 32
GROUP = 4
ROWS = SIDE // TY
COLS = SIDE // TX


def basis_table(basis):
    kernels, width = basis.shape[0], basis.shape[1]
    w = np.arange(WIN)[:, None] - np.arange(TX)[None, :]
    wide = jnp.pad(basis.astype(jnp.float32), ((0, 0), (0, 0), (0, 1)), constant_values=0.0)
    index = np.where((w >= 0) & (w < width), w, width)
    hot = (index[None] == np.arange(width)[:, None, None]).astype(np.float32)
    table = jnp.einsum("bij,jwt->iwbt", basis.astype(jnp.bfloat16), jnp.asarray(hot, jnp.bfloat16), preferred_element_type=jnp.float32)
    table = table.reshape(width * WIN, kernels * TX).astype(jnp.bfloat16)
    return jnp.concatenate([table, table], axis=1)


def pick_table(pad):
    p = np.arange(TY)
    x = np.arange(SIDE)
    X = np.arange(COLS)
    w = np.arange(WIN)
    keep = (w < TX + 2 * pad)[None, None, None, None, :]
    hit = (p[:, None, None, None, None] == p[None, None, None, :, None]) & (
        x[None, :, None, None, None] == TX * X[None, None, :, None, None] + w[None, None, None, None, :] - pad) & keep
    return hit.reshape(TY * SIDE, COLS * TY * WIN)


def grids():
    g = (2.0 * np.arange(SIDE) + 1.0 - SIDE) / SIDE
    lane = np.arange(128)
    h, q, t = lane // 32, (lane // 8) % 4, lane % 8
    gx = np.stack([g[8 * (4 * h + lo) + t] for lo in range(4)])
    gy = g[4 * np.arange(ROWS)[:, None] + q[None, :]]
    return np.concatenate([gy, np.pad(gx, ((0, 4), (0, 0)))]).astype(np.float32)


def kernel(width, perm, dest, span, shift, *refs):
    coefs, images, taps, ltab, stab, gtab, before, slots, squares, wpad, qf, qb, oscr, zscr, held, sems = refs
    step = pl.program_id(0)
    first, last = span[0], span[1]
    turn = lax.rem(step, 2)

    def place(s, b):
        return jnp.minimum(first + s * GROUP + b, perm.shape[0] - 1)

    def live(s, b):
        return first + s * GROUP + b < last

    def copy(s, b):
        spot = lax.rem(s, 2)
        return pltpu.make_async_copy(held.at[spot, b], slots.at[dest[place(s, b)]], sems.at[spot, b])

    def finish(s):
        for b in range(GROUP):
            @pl.when(live(s, b))
            def _():
                copy(s, b).wait()

    halo = width // 2
    groups = (TY + width - 1) // TY
    rlen = 40
    base = 12

    @pl.when(step == 0)
    def _():
        wpad[...] = jnp.zeros_like(wpad)
        squares[...] = before[...]

    @pl.when(jnp.logical_and(step >= 2, first + step * GROUP < last))
    def _():
        finish(step - 2)

    chosen = [perm[place(step, b)] for b in range(GROUP)]
    @pl.when(first + step * GROUP < last)
    def _():
        delta = lax.broadcasted_iota(jnp.int32, (SIDE, SIDE), 0) - lax.broadcasted_iota(jnp.int32, (SIDE, SIDE), 1)
        lane = lax.broadcasted_iota(jnp.int32, (8, 128), 1)

        def band(b, d):
            off = delta - (shift[chosen[b] * 2 + d] - 3)
            total = jnp.zeros((SIDE, SIDE), jnp.float32)
            for k in range(8):
                total = jnp.where(off == k, taps[chosen[b], d, k][None, :], total)
            return total.astype(jnp.bfloat16)

        kernels = ltab.shape[1] // (2 * TX)
        lanes = lax.broadcasted_iota(jnp.int32, (TX, 128), 1)
        same = lax.broadcasted_iota(jnp.int32, (TX, 128), 0) == lanes % TX

        def weights_of(b):
            at = chosen[b] * 3 * kernels
            wide = [jnp.where(same, jnp.where(lanes < 32, coefs[at + i], jnp.where(lanes < 64, coefs[at + kernels + i], coefs[at + 2 * kernels + i])), 0.0) for i in range(kernels)]
            wide = jnp.concatenate(wide, axis=0)
            high = wide.astype(jnp.bfloat16)
            low = (wide - high.astype(jnp.float32)).astype(jnp.bfloat16)
            return jnp.concatenate([high, low], axis=0)

        picked = []
        for b in range(GROUP):
            half = lax.dot_general(band(b, 0), images[chosen[b]], (((0,), (0,)), ((), ())), preferred_element_type=jnp.float32).astype(jnp.bfloat16)
            warped = jnp.dot(half, band(b, 1), preferred_element_type=jnp.float32)
            wpad[b, base:base + SIDE, :] = warped
            phases = [wpad[b, pl.ds(p + base - halo, rlen, stride=TY), :].astype(jnp.bfloat16) for p in range(TY)]
            picked.append(jnp.concatenate(phases, axis=1))
        lhs = jnp.concatenate(picked, axis=0)
        for X in range(0, COLS, 2):
            got = jnp.dot(lhs, stab[:, 128 * X:128 * X + 256], preferred_element_type=jnp.float32)
            for b in range(GROUP):
                for side in range(2):
                    qf[b, pl.ds(X + side, rlen, stride=COLS), :] = got[b * rlen:(b + 1) * rlen, 128 * side:128 * side + 128]
        qsub = (lax.broadcasted_iota(jnp.int32, (WIN, 128), 1) // TX) % TY
        group_of = (lane // 32)[:1]
        sub_of = ((lane // 8) % 4)[:1]

        def choose(which, values):
            result = values[3]
            for i in (2, 1, 0):
                result = jnp.where(which == i, values[i], result)
            return result

        ltable = ltab[...]
        for pair in range(0, GROUP, 2):
            rr = jnp.concatenate([weights_of(pair), weights_of(pair + 1)], axis=1)
            hh = jnp.dot(ltable, rr, preferred_element_type=jnp.float32)
            for b in (pair, pair + 1):
                qb[b] = qf[b].astype(jnp.bfloat16)
                h = hh[:, 128 * (b - pair):128 * (b - pair) + 128]
                zero = jnp.zeros((WIN, 128), jnp.float32)
                parts = []
                for ii in range(width + TY - 1):
                    rows = [h[WIN * (ii - q):WIN * (ii - q) + WIN] if 0 <= ii - q < width else zero for q in range(TY)]
                    parts.append(choose(qsub, rows).astype(jnp.bfloat16))
                weights = jnp.concatenate(parts, axis=0)
                left = jnp.concatenate([qb[b, COLS * g:COLS * g + ROWS * COLS, :] for g in range(groups)], axis=1)
                oscr[b] = jnp.dot(left, weights, preferred_element_type=jnp.float32)
        summed = jnp.zeros((8, 128), jnp.float32)
        for b in range(GROUP):
            mixed = []
            for lo in range(4):
                a = [oscr[b, pl.ds(4 * h + lo, ROWS, stride=COLS), :] for h in range(4)]
                turned = []
                for k in range(4):
                    diag = choose(group_of, [a[(g + k) % 4] for g in range(4)])
                    turned.append(diag if k == 0 else pltpu.roll(diag, 32 * k, 1))
                m = [choose(group_of, [turned[(h - d) % 4] for h in range(4)]) for d in range(3)]
                mixed.append(m[0] + gtab[ROWS + lo:ROWS + lo + 1, :] * m[1] + gtab[:ROWS, :] * m[2])
            turned = []
            for k in range(4):
                diag = choose(sub_of, [mixed[(g + k) % 4] for g in range(4)])
                if k == 0:
                    turned.append(diag)
                else:
                    turned.append(jnp.where(sub_of >= k, pltpu.roll(diag, 8 * k, 1), pltpu.roll(diag, (8 * k - 32) % 128, 1)))
            total = jnp.zeros((8, 128), jnp.float32)
            for q in range(4):
                final = choose(sub_of, [turned[(lo - q) % 4] for lo in range(4)])
                zscr[b, pl.ds(q, ROWS, stride=TY), :] = final
                sq = final * final
                total = total + (sq[0:8] + sq[8:16] + sq[16:24] + sq[24:32])
            held[turn, b] = zscr[b].astype(jnp.bfloat16)
            summed = summed + jnp.where(live(step, b), total, 0.0)

        squares[...] += summed
        for b in range(GROUP):
            @pl.when(live(step, b))
            def _():
                copy(step, b).start()

        @pl.when(first + (step + 1) * GROUP >= last)
        def _():
            @pl.when(step >= 1)
            def _():
                finish(step - 1)
            finish(step)


def whole(a):
    return pl.BlockSpec(a.shape, lambda s, *_: (0,) * a.ndim)


def match(perm, dest, span, most, tables, images, warp_taps, shift, coefs, before, slots):
    count = images.shape[0]
    width = tables[0].shape[0] // WIN
    given = (images, warp_taps, *tables, before)
    grid_spec = pltpu.PrefetchScalarGridSpec(
        num_scalar_prefetch=5,
        grid=((most + GROUP - 1) // GROUP,),
        in_specs=[pl.BlockSpec(memory_space=pltpu.VMEM) for _ in given],
        out_specs=[
            pl.BlockSpec(memory_space=pl.ANY),
            pl.BlockSpec((8, 128), lambda s, *_: (0, 0)),
        ],
        scratch_shapes=[
            pltpu.VMEM((GROUP, 168, SIDE), jnp.float32),
            pltpu.VMEM((GROUP, 640, 128), jnp.float32),
            pltpu.VMEM((GROUP, 640, 128), jnp.bfloat16),
            pltpu.VMEM((GROUP, 512, 128), jnp.float32),
            pltpu.VMEM((GROUP, 128, 128), jnp.float32),
            pltpu.VMEM((2, GROUP, 128, 128), jnp.bfloat16),
            pltpu.SemaphoreType.DMA((2, GROUP)),
        ],
    )
    return pl.pallas_call(
        functools.partial(kernel, width),
        out_shape=(jax.ShapeDtypeStruct((slots, SIDE, SIDE), jnp.bfloat16), jax.ShapeDtypeStruct((8, 128), jnp.float32)),
        grid_spec=grid_spec,
        compiler_params=pltpu.CompilerParams(vmem_limit_bytes=56 * 1024 * 1024),
        cost_estimate=pl.CostEstimate(flops=40_000_000_000, bytes_accessed=8_000_000, transcendentals=0),
    )(perm, dest, span, shift, coefs, *given)


CHUNK = 16


def gather_sum(labels, scale, step, blocks, total):
    for i in range(CHUNK):
        tile = labels[step * CHUNK + i]

        @pl.when(tile >= 0)
        def _():
            total[tile] += scale[step * CHUNK + i] * blocks[i].astype(jnp.float32)


def spread_out(labels, step, templates, out):
    for i in range(CHUNK):
        tile = labels[step * CHUNK + i]

        @pl.when(tile >= 0)
        def _():
            out[i] = templates[tile]


def partial_kernel(labels, scale, blocks, total):
    step = pl.program_id(0)

    @pl.when(step == 0)
    def _():
        total[...] = jnp.zeros_like(total)

    gather_sum(labels, scale, step, blocks, total)


def coadd_kernel(labels, scale, inverse, blocks, earlier, coadd, templates, out, arrived, total, done, small, leaving, sems):
    parts = arrived.shape[0] // CHUNK
    taken = [pltpu.make_async_copy(earlier, total, sems.at[0])]
    given = [pltpu.make_async_copy(done, coadd, sems.at[1]), pltpu.make_async_copy(small, templates, sems.at[2])]
    for i in range(parts):
        part = pl.ds(i * CHUNK, CHUNK)
        taken.append(pltpu.make_async_copy(blocks.at[part], arrived.at[part], sems.at[3 + i]))
        given.append(pltpu.make_async_copy(leaving.at[part], out.at[part], sems.at[3 + parts + i]))
    for copy in taken:
        copy.start()
    taken[0].wait()
    for i in range(parts):
        taken[1 + i].wait()
        gather_sum(labels, scale, i, arrived.at[pl.ds(i * CHUNK, CHUNK)], total)
    for tile in range(PG * PG):
        value = total[tile] * inverse[tile]
        done[tile] = value
        small[tile] = value.astype(jnp.bfloat16)
    given[0].start()
    given[1].start()
    for i in range(parts):
        spread_out(labels, i, small, leaving.at[pl.ds(i * CHUNK, CHUNK)])
        given[2 + i].start()
    for copy in given:
        copy.wait()


def spread_kernel(labels, templates, out):
    spread_out(labels, pl.program_id(0), templates, out)


def slots_spec(where):
    return pl.BlockSpec((CHUNK, SIDE, SIDE), lambda s, *_: (where(s), 0, 0))


def partial_sum(labels, scale, blocks):
    tiles = (PG * PG, SIDE, SIDE)
    return pl.pallas_call(
        partial_kernel,
        out_shape=jax.ShapeDtypeStruct(tiles, jnp.float32),
        grid_spec=pltpu.PrefetchScalarGridSpec(
            num_scalar_prefetch=2, grid=(blocks.shape[0] // CHUNK,),
            in_specs=[slots_spec(lambda s: s)],
            out_specs=pl.BlockSpec(tiles, lambda s, *_: (0, 0, 0))),
        cost_estimate=pl.CostEstimate(flops=1_000, bytes_accessed=1_000, transcendentals=0),
    )(labels, scale, blocks)


def finish_sum(labels, scale, inverse, blocks, earlier):
    tiles = (PG * PG, SIDE, SIDE)
    anywhere = pl.BlockSpec(memory_space=pl.ANY)
    return pl.pallas_call(
        coadd_kernel,
        out_shape=(jax.ShapeDtypeStruct(tiles, jnp.float32), jax.ShapeDtypeStruct(tiles, jnp.bfloat16), jax.ShapeDtypeStruct(blocks.shape, jnp.bfloat16)),
        grid_spec=pltpu.PrefetchScalarGridSpec(
            num_scalar_prefetch=3, grid=(1,),
            in_specs=[anywhere, anywhere],
            out_specs=[anywhere, anywhere, anywhere],
            scratch_shapes=[
                pltpu.VMEM(blocks.shape, jnp.bfloat16),
                pltpu.VMEM(tiles, jnp.float32),
                pltpu.VMEM(tiles, jnp.float32),
                pltpu.VMEM(tiles, jnp.bfloat16),
                pltpu.VMEM(blocks.shape, jnp.bfloat16),
                pltpu.SemaphoreType.DMA((3 + 2 * (blocks.shape[0] // CHUNK),)),
            ]),
        compiler_params=pltpu.CompilerParams(vmem_limit_bytes=60 * 1024 * 1024),
        cost_estimate=pl.CostEstimate(flops=10_000_000, bytes_accessed=10_000_000, transcendentals=0),
    )(labels, scale, inverse, blocks, earlier)


def spread(labels, templates, slots):
    return pl.pallas_call(
        spread_kernel,
        out_shape=jax.ShapeDtypeStruct((slots, SIDE, SIDE), jnp.bfloat16),
        grid_spec=pltpu.PrefetchScalarGridSpec(
            num_scalar_prefetch=1, grid=(slots // CHUNK,),
            in_specs=[pl.BlockSpec(templates.shape, lambda s, *_: (0, 0, 0))],
            out_specs=slots_spec(lambda s: s)),
        cost_estimate=pl.CostEstimate(flops=10_000_000, bytes_accessed=5_000_000, transcendentals=0),
    )(labels, templates)


def first_diff_kernel(perm, dest, span, sent, template, out):
    out[...] = sent[...].astype(jnp.float32) - template[...].astype(jnp.float32)


def second_diff_kernel(perm, dest, span, sent, template, held, out, left, right, answer, sems):
    most = left.shape[0]
    number = jnp.minimum(span[1], most)

    def copies(i):
        return (pltpu.make_async_copy(sent.at[dest[i]], left.at[i], sems.at[0, i]), pltpu.make_async_copy(template.at[dest[i]], right.at[i], sems.at[1, i]),
                pltpu.make_async_copy(answer.at[i], out.at[perm[i]], sems.at[2, i]))

    @pl.loop(0, number)
    def _(i):
        first, second, _ = copies(i)
        first.start()
        second.start()

    @pl.loop(0, number)
    def _(i):
        first, second, third = copies(i)
        first.wait()
        second.wait()
        answer[i] = left[i].astype(jnp.float32) - right[i].astype(jnp.float32)
        third.start()

    @pl.loop(0, number)
    def _(i):
        copies(i)[2].wait()


def subtract(perm, dest, span, most, sent, template):
    count = perm.shape[0]
    at = lambda s, span: jnp.maximum(jnp.minimum(span[0] + s, span[1] - 1), 0)
    one = (1, SIDE, SIDE)
    slot = pl.BlockSpec(one, lambda s, perm, dest, span: (dest[at(s, span)], 0, 0))
    row = pl.BlockSpec(one, lambda s, perm, dest, span: (perm[at(s, span)], 0, 0))
    return pl.pallas_call(
        first_diff_kernel,
        out_shape=jax.ShapeDtypeStruct((count, SIDE, SIDE), jnp.float32),
        grid_spec=pltpu.PrefetchScalarGridSpec(
            num_scalar_prefetch=3, grid=(most,), in_specs=[slot, slot], out_specs=row),
        cost_estimate=pl.CostEstimate(flops=10_000_000, bytes_accessed=8_000_000, transcendentals=0),
    )(perm, dest, span, sent, template)


def subtract_rest(perm, dest, span, most, sent, template, held):
    anywhere = pl.BlockSpec(memory_space=pl.ANY)
    return pl.pallas_call(
        second_diff_kernel,
        out_shape=jax.ShapeDtypeStruct(held.shape, held.dtype),
        grid_spec=pltpu.PrefetchScalarGridSpec(
            num_scalar_prefetch=3, grid=(1,), in_specs=[anywhere] * 3, out_specs=anywhere,
            scratch_shapes=[
                pltpu.VMEM((most, SIDE, SIDE), jnp.bfloat16),
                pltpu.VMEM((most, SIDE, SIDE), jnp.bfloat16),
                pltpu.VMEM((most, SIDE, SIDE), jnp.float32),
                pltpu.SemaphoreType.DMA((3, most)),
            ]),
        input_output_aliases={5: 0},
        compiler_params=pltpu.CompilerParams(vmem_limit_bytes=56 * 1024 * 1024),
        cost_estimate=pl.CostEstimate(flops=1_000_000, bytes_accessed=2_000_000, transcendentals=0),
    )(perm, dest, span, sent, template, held)


def body(images, warp_taps, warp_shift, psf_coefs, psf_basis, owner, offsets):
    axes = ("visit", "det")
    count = images.shape[0]
    n_visit, n_det = (lax.axis_size("visit"), lax.axis_size("det"))
    devices = n_visit * n_det
    target = owner[:, 0]
    tile = offsets[:, 0] * PG + offsets[:, 1]
    order = jnp.arange(count, dtype=jnp.int32)
    second = jnp.any((target[:, None] == target[None, :]) & (order[:, None] > order[None, :]), axis=1)
    seconds = jnp.sum(second.astype(jnp.int32))
    before_me = order[None, :] < order[:, None]
    lower = jnp.sum((before_me & (second[None, :] == second[:, None])).astype(jnp.int32), axis=1)
    position = jnp.where(second, lower, seconds + lower)
    put = position[None, :] == order[:, None]
    perm = jnp.sum(jnp.where(put, order[None, :], 0), axis=1)
    dest = jnp.sum(jnp.where(put, target[None, :], 0), axis=1)
    zero = jnp.zeros((), jnp.int32)
    span_second = jnp.stack([zero, seconds])
    span_first = jnp.stack([seconds, zero + count])

    tables = (basis_table(psf_basis), jnp.asarray(pick_table(psf_basis.shape[1] // 2), jnp.bfloat16), jnp.asarray(grids()))
    ours = (images, warp_taps, warp_shift.reshape(-1), psf_coefs.reshape(-1))
    exchange = lambda a: lax.all_to_all(a, axes, split_axis=0, concat_axis=0, tiled=True)
    out_second, squares = match(perm, dest, span_second, count // 2, tables, *ours, jnp.zeros((8, 128), jnp.float32), devices)
    in_second = exchange(out_second)
    out_first, squares = match(perm, dest, span_first, count, tables, *ours, squares, devices)
    in_second, out_first, squares = lax.optimization_barrier((in_second, out_first, squares))
    named = target[None, :] == jnp.arange(devices, dtype=jnp.int32)[:, None]
    label = lambda rank: jnp.max(jnp.where(named & (second == rank)[None, :], tile[None, :], -1), axis=1).astype(jnp.float32)
    note = jnp.stack([jnp.full((devices,), jnp.sum(squares)), label(False), label(True)], axis=1)
    notes = exchange(note)
    in_first = exchange(out_first)
    power = notes[:, 0].reshape(n_visit, n_det).sum(axis=1)
    entries = count * SIDE * SIDE * n_det
    weight = lax.reduce_precision(1.0 / (power / entries + 1e-06), 8, 7)
    scale = jnp.repeat(weight, n_det)
    label_first, label_second = notes[:, 1].astype(jnp.int32), notes[:, 2].astype(jnp.int32)
    kinds = jnp.arange(PG * PG, dtype=jnp.int32)[:, None]
    hits = (label_first[None] == kinds).astype(jnp.float32) + (label_second[None] == kinds).astype(jnp.float32)
    inverse = 1.0 / jnp.maximum(jnp.sum(hits * scale[None], axis=1), 0.25)

    earlier = partial_sum(label_second, scale, in_second)
    coadd, templates, back_first = finish_sum(label_first, scale, inverse, in_first, earlier)
    home_first = exchange(back_first)
    home_second = exchange(spread(label_second, templates, devices))
    difference = subtract(perm, dest, span_first, count, out_first, home_first)
    difference = subtract_rest(perm, dest, span_second, count // 2, out_second, home_second, difference)
    return (difference, coadd)


def solution(mesh):
    in_specs = (
        P(("visit", "det"), None, None),
        P(("visit", "det"), None, None, None),
        P(("visit", "det"), None),
        P(("visit", "det"), None, None),
        P(),
        P(("visit", "det"), None),
        P(("visit", "det"), None),
    )
    out_specs = (P(("visit", "det"), None, None), P(("visit", "det"), None, None))
    return jax.shard_map(body, mesh=mesh, in_specs=in_specs, out_specs=out_specs, check_vma=False)
```

```python
import functools

import jax
import jax.numpy as jnp
import numpy as np
from jax import lax
from jax.experimental import pallas as pl
from jax.experimental.pallas import tpu as pltpu
from jax.sharding import PartitionSpec as P

PG = 4
SIDE = 128
TX = 8
TY = 4
WIN = 32
GROUP = 4
ROWS = SIDE // TY
COLS = SIDE // TX


def basis_table(basis):
    kernels, width = basis.shape[0], basis.shape[1]
    w = np.arange(WIN)[:, None] - np.arange(TX)[None, :]
    wide = jnp.pad(basis.astype(jnp.float32), ((0, 0), (0, 0), (0, 1)), constant_values=0.0)
    index = np.where((w >= 0) & (w < width), w, width)
    hot = (index[None] == np.arange(width)[:, None, None]).astype(np.float32)
    table = jnp.einsum("bij,jwt->iwbt", basis.astype(jnp.bfloat16), jnp.asarray(hot, jnp.bfloat16), preferred_element_type=jnp.float32)
    table = table.reshape(width * WIN, kernels * TX).astype(jnp.bfloat16)
    return jnp.concatenate([table, table], axis=1)


def pick_table(pad):
    p = np.arange(TY)
    x = np.arange(SIDE)
    X = np.arange(COLS)
    w = np.arange(WIN)
    keep = (w < TX + 2 * pad)[None, None, None, None, :]
    hit = (p[:, None, None, None, None] == p[None, None, None, :, None]) & (
        x[None, :, None, None, None] == TX * X[None, None, :, None, None] + w[None, None, None, None, :] - pad) & keep
    return hit.reshape(TY * SIDE, COLS * TY * WIN)


def grids():
    g = (2.0 * np.arange(SIDE) + 1.0 - SIDE) / SIDE
    lane = np.arange(128)
    h, q, t = lane // 32, (lane // 8) % 4, lane % 8
    gx = np.stack([g[8 * (4 * h + lo) + t] for lo in range(4)])
    gy = g[4 * np.arange(ROWS)[:, None] + q[None, :]]
    return np.concatenate([gy, np.pad(gx, ((0, 4), (0, 0)))]).astype(np.float32)


def kernel(width, halves, perm, dest, span, top, bottom, third, shift, *refs):
    coefs, images, taps, ltab, stab, gtab, before, slots = refs[:8]
    spare = refs[8] if halves else None
    squares, wpad, qf, qb, oscr, zscr, held, sems = refs[-8:]
    step = pl.program_id(0)
    first, last = span[0], span[1]
    turn = lax.rem(step, 2)

    def place(s, b):
        return jnp.minimum(first + s * GROUP + b, perm.shape[0] - 1)

    def live(s, b):
        return first + s * GROUP + b < last

    def copies(s, b, act):
        spot, at = lax.rem(s, 2), place(s, b)
        if not halves:
            @pl.when(live(s, b))
            def _():
                act(pltpu.make_async_copy(held.at[spot, b], slots.at[dest[at]], sems.at[spot, b, 0]))
        else:
            @pl.when(jnp.logical_and(live(s, b), third[at] == 0))
            def _():
                for side, slot in enumerate((top[at], bottom[at])):
                    part = held.at[spot, b, pl.ds(side * SIDE // 2, SIDE // 2)]
                    act(pltpu.make_async_copy(part, slots.at[slot], sems.at[spot, b, side]))

            @pl.when(jnp.logical_and(live(s, b), third[at] == 1))
            def _():
                act(pltpu.make_async_copy(held.at[spot, b], spare.at[dest[at]], sems.at[spot, b, 0]))

    def finish(s):
        for b in range(GROUP):
            copies(s, b, lambda one: one.wait())

    halo = width // 2
    groups = (TY + width - 1) // TY
    rlen = 40
    base = 12

    @pl.when(step == 0)
    def _():
        wpad[...] = jnp.zeros_like(wpad)
        squares[...] = before[...]

    @pl.when(jnp.logical_and(step >= 2, first + step * GROUP < last))
    def _():
        finish(step - 2)

    chosen = [perm[place(step, b)] for b in range(GROUP)]
    @pl.when(first + step * GROUP < last)
    def _():
        delta = lax.broadcasted_iota(jnp.int32, (SIDE, SIDE), 0) - lax.broadcasted_iota(jnp.int32, (SIDE, SIDE), 1)
        lane = lax.broadcasted_iota(jnp.int32, (8, 128), 1)

        def band(b, d):
            off = delta - (shift[chosen[b] * 2 + d] - 3)
            total = jnp.zeros((SIDE, SIDE), jnp.float32)
            for k in range(8):
                total = jnp.where(off == k, taps[chosen[b], d, k][None, :], total)
            return total.astype(jnp.bfloat16)

        kernels = ltab.shape[1] // (2 * TX)
        lanes = lax.broadcasted_iota(jnp.int32, (TX, 128), 1)
        same = lax.broadcasted_iota(jnp.int32, (TX, 128), 0) == lanes % TX

        def weights_of(b):
            at = chosen[b] * 3 * kernels
            wide = [jnp.where(same, jnp.where(lanes < 32, coefs[at + i], jnp.where(lanes < 64, coefs[at + kernels + i], coefs[at + 2 * kernels + i])), 0.0) for i in range(kernels)]
            wide = jnp.concatenate(wide, axis=0)
            high = wide.astype(jnp.bfloat16)
            low = (wide - high.astype(jnp.float32)).astype(jnp.bfloat16)
            return jnp.concatenate([high, low], axis=0)

        picked = []
        for b in range(GROUP):
            half = lax.dot_general(band(b, 0), images[chosen[b]], (((0,), (0,)), ((), ())), preferred_element_type=jnp.float32).astype(jnp.bfloat16)
            warped = jnp.dot(half, band(b, 1), preferred_element_type=jnp.float32)
            wpad[b, base:base + SIDE, :] = warped
            phases = [wpad[b, pl.ds(p + base - halo, rlen, stride=TY), :].astype(jnp.bfloat16) for p in range(TY)]
            picked.append(jnp.concatenate(phases, axis=1))
        lhs = jnp.concatenate(picked, axis=0)
        for X in range(0, COLS, 2):
            got = jnp.dot(lhs, stab[:, 128 * X:128 * X + 256], preferred_element_type=jnp.float32)
            for b in range(GROUP):
                for side in range(2):
                    qf[b, pl.ds(X + side, rlen, stride=COLS), :] = got[b * rlen:(b + 1) * rlen, 128 * side:128 * side + 128]
        qsub = (lax.broadcasted_iota(jnp.int32, (WIN, 128), 1) // TX) % TY
        group_of = (lane // 32)[:1]
        sub_of = ((lane // 8) % 4)[:1]

        def choose(which, values):
            result = values[3]
            for i in (2, 1, 0):
                result = jnp.where(which == i, values[i], result)
            return result

        ltable = ltab[...]
        for pair in range(0, GROUP, 2):
            rr = jnp.concatenate([weights_of(pair), weights_of(pair + 1)], axis=1)
            hh = jnp.dot(ltable, rr, preferred_element_type=jnp.float32)
            for b in (pair, pair + 1):
                qb[b] = qf[b].astype(jnp.bfloat16)
                h = hh[:, 128 * (b - pair):128 * (b - pair) + 128]
                zero = jnp.zeros((WIN, 128), jnp.float32)
                parts = []
                for ii in range(width + TY - 1):
                    rows = [h[WIN * (ii - q):WIN * (ii - q) + WIN] if 0 <= ii - q < width else zero for q in range(TY)]
                    parts.append(choose(qsub, rows).astype(jnp.bfloat16))
                weights = jnp.concatenate(parts, axis=0)
                left = jnp.concatenate([qb[b, COLS * g:COLS * g + ROWS * COLS, :] for g in range(groups)], axis=1)
                oscr[b] = jnp.dot(left, weights, preferred_element_type=jnp.float32)
        summed = jnp.zeros((8, 128), jnp.float32)
        for b in range(GROUP):
            mixed = []
            for lo in range(4):
                a = [oscr[b, pl.ds(4 * h + lo, ROWS, stride=COLS), :] for h in range(4)]
                turned = []
                for k in range(4):
                    diag = choose(group_of, [a[(g + k) % 4] for g in range(4)])
                    turned.append(diag if k == 0 else pltpu.roll(diag, 32 * k, 1))
                m = [choose(group_of, [turned[(h - d) % 4] for h in range(4)]) for d in range(3)]
                mixed.append(m[0] + gtab[ROWS + lo:ROWS + lo + 1, :] * m[1] + gtab[:ROWS, :] * m[2])
            turned = []
            for k in range(4):
                diag = choose(sub_of, [mixed[(g + k) % 4] for g in range(4)])
                if k == 0:
                    turned.append(diag)
                else:
                    turned.append(jnp.where(sub_of >= k, pltpu.roll(diag, 8 * k, 1), pltpu.roll(diag, (8 * k - 32) % 128, 1)))
            total = jnp.zeros((8, 128), jnp.float32)
            for q in range(4):
                final = choose(sub_of, [turned[(lo - q) % 4] for lo in range(4)])
                zscr[b, pl.ds(q, ROWS, stride=TY), :] = final
                sq = final * final
                total = total + (sq[0:8] + sq[8:16] + sq[16:24] + sq[24:32])
            held[turn, b] = zscr[b].astype(jnp.bfloat16)
            summed = summed + jnp.where(live(step, b), total, 0.0)

        squares[...] += summed
        for b in range(GROUP):
            copies(step, b, lambda one: one.start())

        @pl.when(first + (step + 1) * GROUP >= last)
        def _():
            @pl.when(step >= 1)
            def _():
                finish(step - 1)
            finish(step)


def whole(a):
    return pl.BlockSpec(a.shape, lambda s, *_: (0,) * a.ndim)


def match(lists, halves, most, tables, images, warp_taps, shift, coefs, before, slots):
    count = images.shape[0]
    width = tables[0].shape[0] // WIN
    given = (images, warp_taps, *tables, before)
    sizes = [(slots, SIDE // 2, SIDE), (slots, SIDE, SIDE)] if halves else [(slots, SIDE, SIDE)]
    grid_spec = pltpu.PrefetchScalarGridSpec(
        num_scalar_prefetch=8,
        grid=((most + GROUP - 1) // GROUP,),
        in_specs=[pl.BlockSpec(memory_space=pltpu.VMEM) for _ in given],
        out_specs=[pl.BlockSpec(memory_space=pl.ANY) for _ in sizes] + [
            pl.BlockSpec((8, 128), lambda s, *_: (0, 0)),
        ],
        scratch_shapes=[
            pltpu.VMEM((GROUP, 168, SIDE), jnp.float32),
            pltpu.VMEM((GROUP, 640, 128), jnp.float32),
            pltpu.VMEM((GROUP, 640, 128), jnp.bfloat16),
            pltpu.VMEM((GROUP, 512, 128), jnp.float32),
            pltpu.VMEM((GROUP, 128, 128), jnp.float32),
            pltpu.VMEM((2, GROUP, 128, 128), jnp.bfloat16),
            pltpu.SemaphoreType.DMA((2, GROUP, 2)),
        ],
    )
    return pl.pallas_call(
        functools.partial(kernel, width, halves),
        out_shape=(*[jax.ShapeDtypeStruct(size, jnp.bfloat16) for size in sizes], jax.ShapeDtypeStruct((8, 128), jnp.float32)),
        grid_spec=grid_spec,
        compiler_params=pltpu.CompilerParams(vmem_limit_bytes=56 * 1024 * 1024),
        cost_estimate=pl.CostEstimate(flops=40_000_000_000, bytes_accessed=8_000_000, transcendentals=0),
    )(*lists, shift, coefs, *given)


CHUNK = 16


def gather_sum(labels, scale, step, blocks, total):
    for i in range(CHUNK):
        tile = labels[step * CHUNK + i]

        @pl.when(tile >= 0)
        def _():
            total[tile] += scale[step * CHUNK + i] * blocks[i].astype(jnp.float32)


def spread_out(labels, step, templates, out):
    for i in range(CHUNK):
        tile = labels[step * CHUNK + i]

        @pl.when(tile >= 0)
        def _():
            out[i] = templates[tile]


def partial_kernel(labels, scale, blocks, total):
    step = pl.program_id(0)

    @pl.when(step == 0)
    def _():
        total[...] = jnp.zeros_like(total)

    gather_sum(labels, scale, step, blocks, total)


def coadd_kernel(labels, scale, inverse, blocks, earlier, coadd, templates, out, arrived, total, done, small, leaving, sems):
    parts = arrived.shape[0] // CHUNK
    taken = [pltpu.make_async_copy(earlier, total, sems.at[0])]
    given = [pltpu.make_async_copy(done, coadd, sems.at[1]), pltpu.make_async_copy(small, templates, sems.at[2])]
    for i in range(parts):
        part = pl.ds(i * CHUNK, CHUNK)
        taken.append(pltpu.make_async_copy(blocks.at[part], arrived.at[part], sems.at[3 + i]))
        given.append(pltpu.make_async_copy(leaving.at[part], out.at[part], sems.at[3 + parts + i]))
    for copy in taken:
        copy.start()
    taken[0].wait()
    for i in range(parts):
        taken[1 + i].wait()
        gather_sum(labels, scale, i, arrived.at[pl.ds(i * CHUNK, CHUNK)], total)
    for tile in range(PG * PG):
        value = total[tile] * inverse[tile]
        done[tile] = value
        small[tile] = value.astype(jnp.bfloat16)
    given[0].start()
    given[1].start()
    for i in range(parts):
        spread_out(labels, i, small, leaving.at[pl.ds(i * CHUNK, CHUNK)])
        given[2 + i].start()
    for copy in given:
        copy.wait()


def spread_kernel(labels, templates, out):
    spread_out(labels, pl.program_id(0), templates, out)


def slots_spec(where, height=SIDE):
    return pl.BlockSpec((CHUNK, height, SIDE), lambda s, *_: (where(s), 0, 0))


def partial_sum(labels, scale, blocks, number):
    tiles = (number, blocks.shape[1], SIDE)
    return pl.pallas_call(
        partial_kernel,
        out_shape=jax.ShapeDtypeStruct(tiles, jnp.float32),
        grid_spec=pltpu.PrefetchScalarGridSpec(
            num_scalar_prefetch=2, grid=(blocks.shape[0] // CHUNK,),
            in_specs=[slots_spec(lambda s: s, blocks.shape[1])],
            out_specs=pl.BlockSpec(tiles, lambda s, *_: (0, 0, 0))),
        cost_estimate=pl.CostEstimate(flops=1_000, bytes_accessed=1_000, transcendentals=0),
    )(labels, scale, blocks)


def finish_sum(labels, scale, inverse, blocks, earlier):
    tiles = (PG * PG, SIDE, SIDE)
    anywhere = pl.BlockSpec(memory_space=pl.ANY)
    return pl.pallas_call(
        coadd_kernel,
        out_shape=(jax.ShapeDtypeStruct(tiles, jnp.float32), jax.ShapeDtypeStruct(tiles, jnp.bfloat16), jax.ShapeDtypeStruct(blocks.shape, jnp.bfloat16)),
        grid_spec=pltpu.PrefetchScalarGridSpec(
            num_scalar_prefetch=3, grid=(1,),
            in_specs=[anywhere, anywhere],
            out_specs=[anywhere, anywhere, anywhere],
            scratch_shapes=[
                pltpu.VMEM(blocks.shape, jnp.bfloat16),
                pltpu.VMEM(tiles, jnp.float32),
                pltpu.VMEM(tiles, jnp.float32),
                pltpu.VMEM(tiles, jnp.bfloat16),
                pltpu.VMEM(blocks.shape, jnp.bfloat16),
                pltpu.SemaphoreType.DMA((3 + 2 * (blocks.shape[0] // CHUNK),)),
            ]),
        compiler_params=pltpu.CompilerParams(vmem_limit_bytes=60 * 1024 * 1024),
        cost_estimate=pl.CostEstimate(flops=10_000_000, bytes_accessed=10_000_000, transcendentals=0),
    )(labels, scale, inverse, blocks, earlier)


def spread(labels, templates, slots):
    return pl.pallas_call(
        spread_kernel,
        out_shape=jax.ShapeDtypeStruct((slots,) + templates.shape[1:], jnp.bfloat16),
        grid_spec=pltpu.PrefetchScalarGridSpec(
            num_scalar_prefetch=1, grid=(slots // CHUNK,),
            in_specs=[pl.BlockSpec(templates.shape, lambda s, *_: (0, 0, 0))],
            out_specs=slots_spec(lambda s: s, templates.shape[1])),
        cost_estimate=pl.CostEstimate(flops=10_000_000, bytes_accessed=5_000_000, transcendentals=0),
    )(labels, templates)


def difference_kernel(halves, kind, aliased, perm, dest, span, top, bottom, third, sent, template, *refs):
    out, left, right, answer, sems = refs[1:] if aliased else refs
    begin, number = span[0], span[1] - span[0]
    height = sent.shape[1]

    def each(act):
        @pl.loop(0, number)
        def _(i):
            @pl.when(third[begin + i] == kind)
            def _():
                act(i)

    def inward(i):
        for side in range(SIDE // height):
            slot = (top, bottom)[side][begin + i] if halves else dest[begin + i]
            part = pl.ds(side * height, height)
            yield pltpu.make_async_copy(sent.at[slot], left.at[i, part], sems.at[0, side, i])
            yield pltpu.make_async_copy(template.at[slot], right.at[i, part], sems.at[1, side, i])

    def outward(i):
        return pltpu.make_async_copy(answer.at[i], out.at[perm[begin + i]], sems.at[2, 0, i])

    def fetch(i):
        for one in inward(i):
            one.start()

    def work(i):
        for one in inward(i):
            one.wait()
        answer[i] = left[i].astype(jnp.float32) - right[i].astype(jnp.float32)
        outward(i).start()

    each(fetch)
    each(work)
    each(lambda i: outward(i).wait())


def subtract(lists, halves, kind, most, sent, template, held=None):
    anywhere = pl.BlockSpec(memory_space=pl.ANY)
    more = [] if held is None else [held]
    return pl.pallas_call(
        functools.partial(difference_kernel, halves, kind, held is not None),
        out_shape=jax.ShapeDtypeStruct((lists[0].shape[0], SIDE, SIDE), jnp.float32),
        grid_spec=pltpu.PrefetchScalarGridSpec(
            num_scalar_prefetch=6, grid=(1,), in_specs=[anywhere] * (2 + len(more)), out_specs=anywhere,
            scratch_shapes=[
                pltpu.VMEM((most, SIDE, SIDE), jnp.bfloat16),
                pltpu.VMEM((most, SIDE, SIDE), jnp.bfloat16),
                pltpu.VMEM((most, SIDE, SIDE), jnp.float32),
                pltpu.SemaphoreType.DMA((3, 2, most)),
            ]),
        input_output_aliases={8: 0} if more else {},
        compiler_params=pltpu.CompilerParams(vmem_limit_bytes=56 * 1024 * 1024),
        cost_estimate=pl.CostEstimate(flops=1_000_000, bytes_accessed=2_000_000, transcendentals=0),
    )(*lists, sent, template, *more)


def nothing(out):
    pass


def unused(like):
    return pl.pallas_call(
        nothing,
        out_shape=jax.ShapeDtypeStruct(like.shape, like.dtype),
        out_specs=pl.BlockSpec(memory_space=pl.ANY),
    )()


def body(images, warp_taps, warp_shift, psf_coefs, psf_basis, owner, offsets):
    axes = ("visit", "det")
    count = images.shape[0]
    n_visit, n_det = (lax.axis_size("visit"), lax.axis_size("det"))
    devices = n_visit * n_det
    target = owner[:, 0]
    tile = offsets[:, 0] * PG + offsets[:, 1]
    order = jnp.arange(count, dtype=jnp.int32)
    second = jnp.any((target[:, None] == target[None, :]) & (order[:, None] > order[None, :]), axis=1)
    seconds = jnp.sum(second.astype(jnp.int32))
    before_me = order[None, :] < order[:, None]
    lower = jnp.sum((before_me & (second[None, :] == second[:, None])).astype(jnp.int32), axis=1)
    position = jnp.where(second, lower, seconds + lower)
    put = position[None, :] == order[:, None]
    perm = jnp.sum(jnp.where(put, order[None, :], 0), axis=1)
    dest = jnp.sum(jnp.where(put, target[None, :], 0), axis=1)
    def partner(device, way):
        visit, det = device // n_det, device % n_det
        return (visit + 1 - 2 * (visit % 2)) * n_det + det if way == 0 else device + 1 - 2 * (det % 2)

    def half_of(device):
        return (device // n_det + device % n_det) % 2

    def clashes(way):
        pair = jnp.minimum(target, partner(target, way))
        return second & jnp.any(second[None, :] & (pair[:, None] == pair[None, :]) & before_me, axis=1)

    clash = [clashes(way) for way in range(2)]
    other_way = jnp.any(clash[0]) & ~jnp.any(clash[1])
    extra = jnp.where(other_way, clash[1], clash[0])
    mate = jnp.where(other_way, partner(target, 1), partner(target, 0))
    lower = half_of(target) == 1
    third, top, bottom = [jnp.sum(jnp.where(put, a[None, :], 0), axis=1) for a in (extra, jnp.where(lower, mate, target), jnp.where(lower, target, mate))]
    zero = jnp.zeros((), jnp.int32)
    span_second = jnp.stack([zero, seconds])
    span_first = jnp.stack([seconds, zero + count])
    lists = lambda span: (perm, dest, span, top, bottom, third)

    tables = (basis_table(psf_basis), jnp.asarray(pick_table(psf_basis.shape[1] // 2), jnp.bfloat16), jnp.asarray(grids()))
    ours = (images, warp_taps, warp_shift.reshape(-1), psf_coefs.reshape(-1))
    exchange = lambda a: lax.all_to_all(a, axes, split_axis=0, concat_axis=0, tiled=True)
    out_second, out_third, squares = match(lists(span_second), True, count // 2, tables, *ours, jnp.zeros((8, 128), jnp.float32), devices)
    in_second = exchange(out_second)
    out_first, squares = match(lists(span_first), False, count, tables, *ours, squares, devices)
    everyone = jnp.arange(devices, dtype=jnp.int32)[:, None]
    label = lambda named, what: jnp.max(jnp.where(named, what, -1), axis=1).astype(jnp.float32)
    here = target[None, :] == everyone
    near = mate[None, :] == everyone
    tiles = PG * PG
    note = jnp.stack([
        label(here & ~second[None, :], tile[None, :]),
        label((here | near) & (second & ~extra)[None, :], tile[None, :] + jnp.where(here, 0, jnp.where(other_way, 2 * tiles, tiles))),
        label(here & extra[None, :], tile[None, :]),
        jnp.full((devices,), jnp.max(extra.astype(jnp.float32))),
        jnp.full((devices,), other_way.astype(jnp.float32)),
        jnp.full((devices,), jnp.sum(squares))], axis=1)
    in_second, out_first, note = lax.optimization_barrier((in_second, out_first, note))
    notes = exchange(note)
    some_third, some_other = jnp.max(notes[:, 3]) > 0, jnp.max(notes[:, 4]) > 0
    in_third = lax.cond(some_third, exchange, unused, out_third)
    in_third, out_first = lax.optimization_barrier((in_third, out_first))
    in_first = exchange(out_first)
    power = notes[:, 5].reshape(n_visit, n_det).sum(axis=1)
    entries = count * SIDE * SIDE * n_det
    weight = lax.reduce_precision(1.0 / (power / entries + 1e-06), 8, 7)
    scale = jnp.repeat(weight, n_det)
    label_first, label_second, label_third = [notes[:, i].astype(jnp.int32) for i in range(3)]

    upper = (lax.axis_index("visit") + lax.axis_index("det")) % 2 == 1
    to_first = lambda a: lax.ppermute(a, "visit", [(v, v ^ 1) for v in range(n_visit)])
    to_second = lambda a: lax.cond(some_other, lambda b: lax.ppermute(b, "det", [(d, d ^ 1) for d in range(n_det)]), lambda b: b, a)
    parts = partial_sum(label_second, scale, in_second, 3 * tiles)
    own = parts[:tiles]
    their = to_first(parts[tiles:2 * tiles]) + to_second(parts[2 * tiles:])
    earlier = jnp.concatenate([jnp.where(upper, their, own), jnp.where(upper, own, their)], axis=1)
    earlier = earlier + partial_sum(label_third, scale, in_third, tiles)
    kinds = jnp.arange(tiles, dtype=jnp.int32)[:, None]
    hits = sum((a[None] == kinds).astype(jnp.float32) for a in (label_first, label_second, label_third))
    inverse = 1.0 / jnp.maximum(jnp.sum(hits * scale[None], axis=1), 0.25)

    coadd, templates, back_first = finish_sum(label_first, scale, inverse, in_first, earlier)
    home_third = lax.cond(some_third, lambda a: exchange(spread(label_third, a, devices)), lambda a: unused(out_third), templates)
    home_third, back_first = lax.optimization_barrier((home_third, back_first))
    home_first = exchange(back_first)
    above, below = templates[:, :SIDE // 2], templates[:, SIDE // 2:]
    across = jnp.where(upper, above, below)
    both = jnp.concatenate([jnp.where(upper, below, above)] + [to_first(across), to_second(across)], axis=0)
    home_second = exchange(spread(label_second, both, devices))
    difference = subtract(lists(span_first), 0, 0, count, out_first, home_first)
    difference = subtract(lists(span_second), 0, 1, count // 2, out_third, home_third, difference)
    difference = subtract(lists(span_second), 1, 0, count // 2, out_second, home_second, difference)
    return (difference, coadd)


def solution(mesh):
    in_specs = (
        P(("visit", "det"), None, None),
        P(("visit", "det"), None, None, None),
        P(("visit", "det"), None),
        P(("visit", "det"), None, None),
        P(),
        P(("visit", "det"), None),
        P(("visit", "det"), None),
    )
    out_specs = (P(("visit", "det"), None, None), P(("visit", "det"), None, None))
    return jax.shard_map(body, mesh=mesh, in_specs=in_specs, out_specs=out_specs, check_vma=False)
```

```python
import functools

import jax
import jax.numpy as jnp
import numpy as np
from jax import lax
from jax.experimental import pallas as pl
from jax.experimental.pallas import tpu as pltpu
from jax.sharding import PartitionSpec as P

PG = 4
SIDE = 128
TX = 8
TY = 4
WIN = 32
GROUP = 4
ROWS = SIDE // TY
COLS = SIDE // TX


def basis_table(basis):
    kernels, width = basis.shape[0], basis.shape[1]
    w = np.arange(WIN)[:, None] - np.arange(TX)[None, :]
    wide = jnp.pad(basis.astype(jnp.float32), ((0, 0), (0, 0), (0, 1)), constant_values=0.0)
    index = np.where((w >= 0) & (w < width), w, width)
    hot = (index[None] == np.arange(width)[:, None, None]).astype(np.float32)
    table = jnp.einsum("bij,jwt->iwbt", basis.astype(jnp.bfloat16), jnp.asarray(hot, jnp.bfloat16), preferred_element_type=jnp.float32)
    table = table.reshape(width * WIN, kernels * TX).astype(jnp.bfloat16)
    return jnp.concatenate([table, table], axis=1)


def pick_table(pad):
    p = np.arange(TY)
    x = np.arange(SIDE)
    X = np.arange(COLS)
    w = np.arange(WIN)
    keep = (w < TX + 2 * pad)[None, None, None, None, :]
    hit = (p[:, None, None, None, None] == p[None, None, None, :, None]) & (
        x[None, :, None, None, None] == TX * X[None, None, :, None, None] + w[None, None, None, None, :] - pad) & keep
    return hit.reshape(TY * SIDE, COLS * TY * WIN)


def grids():
    g = (2.0 * np.arange(SIDE) + 1.0 - SIDE) / SIDE
    lane = np.arange(128)
    h, q, t = lane // 32, (lane // 8) % 4, lane % 8
    gx = np.stack([g[8 * (4 * h + lo) + t] for lo in range(4)])
    gy = g[4 * np.arange(ROWS)[:, None] + q[None, :]]
    return np.concatenate([gy, np.pad(gx, ((0, 4), (0, 0)))]).astype(np.float32)


def kernel(width, halves, perm, dest, span, top, bottom, third, shift, *refs):
    coefs, images, taps, ltab, stab, gtab, before, slots = refs[:8]
    spare = refs[8] if halves else None
    squares, wpad, qf, qb, oscr, zscr, held, sems = refs[-8:]
    step = pl.program_id(0)
    first, last = span[0], span[1]
    turn = lax.rem(step, 2)

    def place(s, b):
        return jnp.minimum(first + s * GROUP + b, perm.shape[0] - 1)

    def live(s, b):
        return first + s * GROUP + b < last

    def copies(s, b, act):
        spot, at = lax.rem(s, 2), place(s, b)
        if not halves:
            @pl.when(live(s, b))
            def _():
                act(pltpu.make_async_copy(held.at[spot, b], slots.at[dest[at]], sems.at[spot, b, 0]))
        else:
            @pl.when(jnp.logical_and(live(s, b), third[at] == 0))
            def _():
                for side, slot in enumerate((top[at], bottom[at])):
                    part = held.at[spot, b, pl.ds(side * SIDE // 2, SIDE // 2)]
                    act(pltpu.make_async_copy(part, slots.at[slot], sems.at[spot, b, side]))

            @pl.when(jnp.logical_and(live(s, b), third[at] == 1))
            def _():
                act(pltpu.make_async_copy(held.at[spot, b], spare.at[dest[at]], sems.at[spot, b, 0]))

    def finish(s):
        for b in range(GROUP):
            copies(s, b, lambda one: one.wait())

    halo = width // 2
    groups = (TY + width - 1) // TY
    rlen = 40
    base = 12

    @pl.when(step == 0)
    def _():
        wpad[...] = jnp.zeros_like(wpad)
        squares[...] = before[...]

    @pl.when(jnp.logical_and(step >= 2, first + step * GROUP < last))
    def _():
        finish(step - 2)

    chosen = [perm[place(step, b)] for b in range(GROUP)]
    @pl.when(first + step * GROUP < last)
    def _():
        delta = lax.broadcasted_iota(jnp.int32, (SIDE, SIDE), 0) - lax.broadcasted_iota(jnp.int32, (SIDE, SIDE), 1)
        lane = lax.broadcasted_iota(jnp.int32, (8, 128), 1)

        def band(b, d):
            off = delta - (shift[chosen[b] * 2 + d] - 3)
            total = jnp.zeros((SIDE, SIDE), jnp.float32)
            for k in range(8):
                total = jnp.where(off == k, taps[chosen[b], d, k][None, :], total)
            return total.astype(jnp.bfloat16)

        kernels = ltab.shape[1] // (2 * TX)
        lanes = lax.broadcasted_iota(jnp.int32, (TX, 128), 1)
        same = lax.broadcasted_iota(jnp.int32, (TX, 128), 0) == lanes % TX

        def weights_of(b):
            at = chosen[b] * 3 * kernels
            wide = [jnp.where(same, jnp.where(lanes < 32, coefs[at + i], jnp.where(lanes < 64, coefs[at + kernels + i], coefs[at + 2 * kernels + i])), 0.0) for i in range(kernels)]
            wide = jnp.concatenate(wide, axis=0)
            high = wide.astype(jnp.bfloat16)
            low = (wide - high.astype(jnp.float32)).astype(jnp.bfloat16)
            return jnp.concatenate([high, low], axis=0)

        picked = []
        for b in range(GROUP):
            half = lax.dot_general(band(b, 0), images[chosen[b]], (((0,), (0,)), ((), ())), preferred_element_type=jnp.float32).astype(jnp.bfloat16)
            warped = jnp.dot(half, band(b, 1), preferred_element_type=jnp.float32)
            wpad[b, base:base + SIDE, :] = warped
            phases = [wpad[b, pl.ds(p + base - halo, rlen, stride=TY), :].astype(jnp.bfloat16) for p in range(TY)]
            picked.append(jnp.concatenate(phases, axis=1))
        lhs = jnp.concatenate(picked, axis=0)
        for X in range(0, COLS, 2):
            got = jnp.dot(lhs, stab[:, 128 * X:128 * X + 256], preferred_element_type=jnp.float32)
            for b in range(GROUP):
                for side in range(2):
                    qf[b, pl.ds(X + side, rlen, stride=COLS), :] = got[b * rlen:(b + 1) * rlen, 128 * side:128 * side + 128]
        qsub = (lax.broadcasted_iota(jnp.int32, (WIN, 128), 1) // TX) % TY
        group_of = (lane // 32)[:1]
        sub_of = ((lane // 8) % 4)[:1]

        def choose(which, values):
            result = values[3]
            for i in (2, 1, 0):
                result = jnp.where(which == i, values[i], result)
            return result

        ltable = ltab[...]
        for pair in range(0, GROUP, 2):
            rr = jnp.concatenate([weights_of(pair), weights_of(pair + 1)], axis=1)
            hh = jnp.dot(ltable, rr, preferred_element_type=jnp.float32)
            for b in (pair, pair + 1):
                qb[b] = qf[b].astype(jnp.bfloat16)
                h = hh[:, 128 * (b - pair):128 * (b - pair) + 128]
                zero = jnp.zeros((WIN, 128), jnp.float32)
                parts = []
                for ii in range(width + TY - 1):
                    rows = [h[WIN * (ii - q):WIN * (ii - q) + WIN] if 0 <= ii - q < width else zero for q in range(TY)]
                    parts.append(choose(qsub, rows).astype(jnp.bfloat16))
                weights = jnp.concatenate(parts, axis=0)
                left = jnp.concatenate([qb[b, COLS * g:COLS * g + ROWS * COLS, :] for g in range(groups)], axis=1)
                oscr[b] = jnp.dot(left, weights, preferred_element_type=jnp.float32)
        summed = jnp.zeros((8, 128), jnp.float32)
        for b in range(GROUP):
            mixed = []
            for lo in range(4):
                a = [oscr[b, pl.ds(4 * h + lo, ROWS, stride=COLS), :] for h in range(4)]
                turned = []
                for k in range(4):
                    diag = choose(group_of, [a[(g + k) % 4] for g in range(4)])
                    turned.append(diag if k == 0 else pltpu.roll(diag, 32 * k, 1))
                m = [choose(group_of, [turned[(h - d) % 4] for h in range(4)]) for d in range(3)]
                mixed.append(m[0] + gtab[ROWS + lo:ROWS + lo + 1, :] * m[1] + gtab[:ROWS, :] * m[2])
            turned = []
            for k in range(4):
                diag = choose(sub_of, [mixed[(g + k) % 4] for g in range(4)])
                if k == 0:
                    turned.append(diag)
                else:
                    turned.append(jnp.where(sub_of >= k, pltpu.roll(diag, 8 * k, 1), pltpu.roll(diag, (8 * k - 32) % 128, 1)))
            total = jnp.zeros((8, 128), jnp.float32)
            for q in range(4):
                final = choose(sub_of, [turned[(lo - q) % 4] for lo in range(4)])
                zscr[b, pl.ds(q, ROWS, stride=TY), :] = final
                sq = final * final
                total = total + (sq[0:8] + sq[8:16] + sq[16:24] + sq[24:32])
            held[turn, b] = zscr[b].astype(jnp.bfloat16)
            summed = summed + jnp.where(live(step, b), total, 0.0)

        squares[...] += summed
        for b in range(GROUP):
            copies(step, b, lambda one: one.start())

        if not halves:
            @pl.when(first + (step + 1) * GROUP >= last)
            def _():
                folded = jnp.sum(jnp.sum(squares[...], axis=0, keepdims=True), axis=1, keepdims=True)
                squares[...] = jnp.broadcast_to(folded, (8, 128))

        @pl.when(first + (step + 1) * GROUP >= last)
        def _():
            @pl.when(step >= 1)
            def _():
                finish(step - 1)
            finish(step)


def whole(a):
    return pl.BlockSpec(a.shape, lambda s, *_: (0,) * a.ndim)


def match(lists, halves, most, tables, images, warp_taps, shift, coefs, before, slots):
    count = images.shape[0]
    width = tables[0].shape[0] // WIN
    given = (images, warp_taps, *tables, before)
    sizes = [(slots, SIDE // 2, SIDE), (slots, SIDE, SIDE)] if halves else [(slots, SIDE, SIDE)]
    grid_spec = pltpu.PrefetchScalarGridSpec(
        num_scalar_prefetch=8,
        grid=((most + GROUP - 1) // GROUP,),
        in_specs=[pl.BlockSpec(memory_space=pltpu.VMEM) for _ in given],
        out_specs=[pl.BlockSpec(memory_space=pl.ANY) for _ in sizes] + [
            pl.BlockSpec((8, 128), lambda s, *_: (0, 0)),
        ],
        scratch_shapes=[
            pltpu.VMEM((GROUP, 168, SIDE), jnp.float32),
            pltpu.VMEM((GROUP, 640, 128), jnp.float32),
            pltpu.VMEM((GROUP, 640, 128), jnp.bfloat16),
            pltpu.VMEM((GROUP, 512, 128), jnp.float32),
            pltpu.VMEM((GROUP, 128, 128), jnp.float32),
            pltpu.VMEM((2, GROUP, 128, 128), jnp.bfloat16),
            pltpu.SemaphoreType.DMA((2, GROUP, 2)),
        ],
    )
    return pl.pallas_call(
        functools.partial(kernel, width, halves),
        out_shape=(*[jax.ShapeDtypeStruct(size, jnp.bfloat16) for size in sizes], jax.ShapeDtypeStruct((8, 128), jnp.float32)),
        grid_spec=grid_spec,
        compiler_params=pltpu.CompilerParams(vmem_limit_bytes=56 * 1024 * 1024),
        cost_estimate=pl.CostEstimate(flops=40_000_000_000, bytes_accessed=8_000_000, transcendentals=0),
    )(*lists, shift, coefs, *given)


CHUNK = 16


def gather_sum(labels, scale, step, blocks, total):
    for i in range(CHUNK):
        tile = labels[step * CHUNK + i]

        @pl.when(tile >= 0)
        def _():
            total[tile] += scale[step * CHUNK + i] * blocks[i].astype(jnp.float32)


def spread_out(labels, step, templates, out):
    for i in range(CHUNK):
        tile = labels[step * CHUNK + i]

        @pl.when(tile >= 0)
        def _():
            out[i] = templates[tile]


def partial_kernel(labels, scale, blocks, total):
    step = pl.program_id(0)

    @pl.when(step == 0)
    def _():
        total[...] = jnp.zeros_like(total)

    gather_sum(labels, scale, step, blocks, total)


def coadd_kernel(labels, scale, inverse, blocks, earlier, coadd, templates, out, arrived, total, done, small, leaving, sems):
    parts = arrived.shape[0] // CHUNK
    taken = [pltpu.make_async_copy(earlier, total, sems.at[0])]
    given = [pltpu.make_async_copy(done, coadd, sems.at[1]), pltpu.make_async_copy(small, templates, sems.at[2])]
    for i in range(parts):
        part = pl.ds(i * CHUNK, CHUNK)
        taken.append(pltpu.make_async_copy(blocks.at[part], arrived.at[part], sems.at[3 + i]))
        given.append(pltpu.make_async_copy(leaving.at[part], out.at[part], sems.at[3 + parts + i]))
    for copy in taken:
        copy.start()
    taken[0].wait()
    for i in range(parts):
        taken[1 + i].wait()
        gather_sum(labels, scale, i, arrived.at[pl.ds(i * CHUNK, CHUNK)], total)
    for tile in range(PG * PG):
        value = total[tile] * inverse[tile]
        done[tile] = value
        small[tile] = value.astype(jnp.bfloat16)
    given[0].start()
    given[1].start()
    for i in range(parts):
        spread_out(labels, i, small, leaving.at[pl.ds(i * CHUNK, CHUNK)])
        given[2 + i].start()
    for copy in given:
        copy.wait()


def spread_kernel(labels, templates, out):
    spread_out(labels, pl.program_id(0), templates, out)


def slots_spec(where, height=SIDE):
    return pl.BlockSpec((CHUNK, height, SIDE), lambda s, *_: (where(s), 0, 0))


def partial_sum(labels, scale, blocks, number):
    tiles = (number, blocks.shape[1], SIDE)
    return pl.pallas_call(
        partial_kernel,
        out_shape=jax.ShapeDtypeStruct(tiles, jnp.float32),
        grid_spec=pltpu.PrefetchScalarGridSpec(
            num_scalar_prefetch=2, grid=(blocks.shape[0] // CHUNK,),
            in_specs=[slots_spec(lambda s: s, blocks.shape[1])],
            out_specs=pl.BlockSpec(tiles, lambda s, *_: (0, 0, 0))),
        cost_estimate=pl.CostEstimate(flops=1_000, bytes_accessed=1_000, transcendentals=0),
    )(labels, scale, blocks)


def finish_sum(labels, scale, inverse, blocks, earlier):
    tiles = (PG * PG, SIDE, SIDE)
    anywhere = pl.BlockSpec(memory_space=pl.ANY)
    return pl.pallas_call(
        coadd_kernel,
        out_shape=(jax.ShapeDtypeStruct(tiles, jnp.float32), jax.ShapeDtypeStruct(tiles, jnp.bfloat16), jax.ShapeDtypeStruct(blocks.shape, jnp.bfloat16)),
        grid_spec=pltpu.PrefetchScalarGridSpec(
            num_scalar_prefetch=3, grid=(1,),
            in_specs=[anywhere, anywhere],
            out_specs=[anywhere, anywhere, anywhere],
            scratch_shapes=[
                pltpu.VMEM(blocks.shape, jnp.bfloat16),
                pltpu.VMEM(tiles, jnp.float32),
                pltpu.VMEM(tiles, jnp.float32),
                pltpu.VMEM(tiles, jnp.bfloat16),
                pltpu.VMEM(blocks.shape, jnp.bfloat16),
                pltpu.SemaphoreType.DMA((3 + 2 * (blocks.shape[0] // CHUNK),)),
            ]),
        compiler_params=pltpu.CompilerParams(vmem_limit_bytes=60 * 1024 * 1024),
        cost_estimate=pl.CostEstimate(flops=10_000_000, bytes_accessed=10_000_000, transcendentals=0),
    )(labels, scale, inverse, blocks, earlier)


def spread(labels, templates, slots):
    return pl.pallas_call(
        spread_kernel,
        out_shape=jax.ShapeDtypeStruct((slots,) + templates.shape[1:], jnp.bfloat16),
        grid_spec=pltpu.PrefetchScalarGridSpec(
            num_scalar_prefetch=1, grid=(slots // CHUNK,),
            in_specs=[pl.BlockSpec(templates.shape, lambda s, *_: (0, 0, 0))],
            out_specs=slots_spec(lambda s: s, templates.shape[1])),
        cost_estimate=pl.CostEstimate(flops=10_000_000, bytes_accessed=5_000_000, transcendentals=0),
    )(labels, templates)


def difference_kernel(halves, kind, near, aliased, perm, dest, span, top, bottom, third, sent, template, *refs):
    out, left, right, answer, sems = refs[1:] if aliased else refs
    begin, number = span[0], span[1] - span[0]
    height = sent.shape[1]

    def each(act):
        @pl.loop(0, number)
        def _(i):
            @pl.when(third[begin + i] == kind)
            def _():
                act(i)

    def inward(i):
        for side in range(SIDE // height):
            slot = (top, bottom)[side][begin + i] if halves else dest[begin + i]
            part = pl.ds(side * height, height)
            yield pltpu.make_async_copy(sent.at[slot], left.at[i, part], sems.at[0, side, i])
            if not near:
                yield pltpu.make_async_copy(template.at[slot], right.at[i, part], sems.at[1, side, i])

    def outward(i):
        return pltpu.make_async_copy(answer.at[i], out.at[perm[begin + i]], sems.at[2, 0, i])

    def fetch(i):
        for one in inward(i):
            one.start()

    def work(i):
        for one in inward(i):
            one.wait()
        if near:
            for side, slot in enumerate((top[begin + i], bottom[begin + i])):
                part = pl.ds(side * height, height)
                answer[i, part] = left[i, part].astype(jnp.float32) - template[slot].astype(jnp.float32)
        else:
            answer[i] = left[i].astype(jnp.float32) - right[i].astype(jnp.float32)
        outward(i).start()

    each(fetch)
    each(work)
    each(lambda i: outward(i).wait())


def subtract(lists, halves, kind, most, sent, template, held=None):
    anywhere = pl.BlockSpec(memory_space=pl.ANY)
    more = [] if held is None else [held]
    near = bool(halves)
    return pl.pallas_call(
        functools.partial(difference_kernel, halves, kind, near, held is not None),
        out_shape=jax.ShapeDtypeStruct((lists[0].shape[0], SIDE, SIDE), jnp.float32),
        grid_spec=pltpu.PrefetchScalarGridSpec(
            num_scalar_prefetch=6, grid=(1,), in_specs=[anywhere, pl.BlockSpec(memory_space=pltpu.VMEM) if near else anywhere] + [anywhere for _ in more], out_specs=anywhere,
            scratch_shapes=[
                pltpu.VMEM((most, SIDE, SIDE), jnp.bfloat16),
                pltpu.VMEM((most, SIDE, SIDE), jnp.bfloat16),
                pltpu.VMEM((most, SIDE, SIDE), jnp.float32),
                pltpu.SemaphoreType.DMA((3, 2, most)),
            ]),
        input_output_aliases={8: 0} if more else {},
        compiler_params=pltpu.CompilerParams(vmem_limit_bytes=56 * 1024 * 1024),
        cost_estimate=pl.CostEstimate(flops=1_000_000, bytes_accessed=2_000_000, transcendentals=0),
    )(*lists, sent, template, *more)


def nothing(out):
    pass


def unused(like):
    return pl.pallas_call(
        nothing,
        out_shape=jax.ShapeDtypeStruct(like.shape, like.dtype),
        out_specs=pl.BlockSpec(memory_space=pl.ANY),
    )()


def body(images, warp_taps, warp_shift, psf_coefs, psf_basis, owner, offsets):
    axes = ("visit", "det")
    count = images.shape[0]
    n_visit, n_det = (lax.axis_size("visit"), lax.axis_size("det"))
    devices = n_visit * n_det
    target = owner[:, 0]
    tile = offsets[:, 0] * PG + offsets[:, 1]
    order = jnp.arange(count, dtype=jnp.int32)
    second = jnp.any((target[:, None] == target[None, :]) & (order[:, None] > order[None, :]), axis=1)
    seconds = jnp.sum(second.astype(jnp.int32))
    before_me = order[None, :] < order[:, None]
    lower = jnp.sum((before_me & (second[None, :] == second[:, None])).astype(jnp.int32), axis=1)
    position = jnp.where(second, lower, seconds + lower)
    put = position[None, :] == order[:, None]
    def partner(device, way):
        visit, det = device // n_det, device % n_det
        return (visit + 1 - 2 * (visit % 2)) * n_det + det if way == 0 else device + 1 - 2 * (det % 2)

    def half_of(device):
        return (device // n_det + device % n_det) % 2

    def clashes(way):
        pair = jnp.minimum(target, partner(target, way))
        return second & jnp.any(second[None, :] & (pair[:, None] == pair[None, :]) & before_me, axis=1)

    clash = [clashes(way) for way in range(2)]
    other_way = jnp.any(clash[0]) & ~jnp.any(clash[1])
    extra = jnp.where(other_way, clash[1], clash[0])
    mate = jnp.where(other_way, partner(target, 1), partner(target, 0))
    lower = half_of(target) == 1
    packed = ((lower.astype(jnp.int32) * 2 + extra.astype(jnp.int32)) * devices + mate) * devices + target
    packed = jnp.sum(jnp.where(put, (packed * count + order)[None, :], 0), axis=1)
    perm, dest, mates = packed % count, packed // count % devices, packed // (count * devices) % devices
    flags = packed // (count * devices * devices)
    third = flags % 2
    top, bottom = jnp.where(flags >= 2, mates, dest), jnp.where(flags >= 2, dest, mates)
    zero = jnp.zeros((), jnp.int32)
    span_second = jnp.stack([zero, seconds])
    span_first = jnp.stack([seconds, zero + count])
    lists = lambda span: (perm, dest, span, top, bottom, third)

    tables = (basis_table(psf_basis), jnp.asarray(pick_table(psf_basis.shape[1] // 2), jnp.bfloat16), jnp.asarray(grids()))
    ours = (images, warp_taps, warp_shift.reshape(-1), psf_coefs.reshape(-1))
    exchange = lambda a: lax.all_to_all(a, axes, split_axis=0, concat_axis=0, tiled=True)
    out_second, out_third, squares = match(lists(span_second), True, count // 2, tables, *ours, jnp.zeros((8, 128), jnp.float32), devices)
    in_second = exchange(out_second)
    out_first, squares = match(lists(span_first), False, count, tables, *ours, squares, devices)
    everyone = jnp.arange(devices, dtype=jnp.int32)[:, None]
    label = lambda named, what: jnp.max(jnp.where(named, what, -1), axis=1).astype(jnp.float32)
    here = target[None, :] == everyone
    near = mate[None, :] == everyone
    tiles = PG * PG
    note = jnp.stack([
        label(here & ~second[None, :], tile[None, :]),
        label((here | near) & (second & ~extra)[None, :], tile[None, :] + jnp.where(here, 0, jnp.where(other_way, 2 * tiles, tiles))),
        label(here & extra[None, :], tile[None, :]),
        jnp.full((devices,), jnp.max(extra.astype(jnp.float32))),
        jnp.full((devices,), other_way.astype(jnp.float32)),
        jnp.full((devices,), squares[0, 0])], axis=1)
    in_second, out_first, note = lax.optimization_barrier((in_second, out_first, note))
    notes = exchange(note)
    some_third, some_other = jnp.max(notes[:, 3]) > 0, jnp.max(notes[:, 4]) > 0
    in_third = lax.cond(some_third, exchange, unused, out_third)
    in_third, out_first = lax.optimization_barrier((in_third, out_first))
    in_first = exchange(out_first)
    power = notes[:, 5].reshape(n_visit, n_det).sum(axis=1)
    entries = count * SIDE * SIDE * n_det
    weight = lax.reduce_precision(1.0 / (power / entries + 1e-06), 8, 7)
    scale = jnp.repeat(weight, n_det)
    label_first, label_second, label_third = [notes[:, i].astype(jnp.int32) for i in range(3)]

    upper = (lax.axis_index("visit") + lax.axis_index("det")) % 2 == 1
    to_first = lambda a: lax.ppermute(a, "visit", [(v, v ^ 1) for v in range(n_visit)])
    to_second = lambda a: lax.cond(some_other, lambda b: lax.ppermute(b, "det", [(d, d ^ 1) for d in range(n_det)]), lambda b: b, a)
    parts = partial_sum(label_second, scale, in_second, 3 * tiles)
    own = parts[:tiles]
    their = to_first(parts[tiles:2 * tiles]) + to_second(parts[2 * tiles:])
    earlier = jnp.concatenate([jnp.where(upper, their, own), jnp.where(upper, own, their)], axis=1)
    earlier = earlier + partial_sum(label_third, scale, in_third, tiles)
    kinds = jnp.arange(tiles, dtype=jnp.int32)[:, None]
    hits = sum((a[None] == kinds).astype(jnp.float32) for a in (label_first, label_second, label_third))
    inverse = 1.0 / jnp.maximum(jnp.sum(hits * scale[None], axis=1), 0.25)

    coadd, templates, back_first = finish_sum(label_first, scale, inverse, in_first, earlier)
    home_third = lax.cond(some_third, lambda a: exchange(spread(label_third, a, devices)), lambda a: unused(out_third), templates)
    home_third, back_first = lax.optimization_barrier((home_third, back_first))
    home_first = exchange(back_first)
    above, below = templates[:, :SIDE // 2], templates[:, SIDE // 2:]
    across = jnp.where(upper, above, below)
    both = jnp.concatenate([jnp.where(upper, below, above)] + [to_first(across), to_second(across)], axis=0)
    home_second = exchange(spread(label_second, both, devices))
    difference = subtract(lists(span_first), 0, 0, count, out_first, home_first)
    difference = subtract(lists(span_second), 0, 1, count // 2, out_third, home_third, difference)
    difference = subtract(lists(span_second), 1, 0, count // 2, out_second, home_second, difference)
    return (difference, coadd)


def solution(mesh):
    in_specs = (
        P(("visit", "det"), None, None),
        P(("visit", "det"), None, None, None),
        P(("visit", "det"), None),
        P(("visit", "det"), None, None),
        P(),
        P(("visit", "det"), None),
        P(("visit", "det"), None),
    )
    out_specs = (P(("visit", "det"), None, None), P(("visit", "det"), None, None))
    return jax.shard_map(body, mesh=mesh, in_specs=in_specs, out_specs=out_specs, check_vma=False)
```

```python
import functools

import jax
import jax.numpy as jnp
import numpy as np
from jax import lax
from jax.experimental import pallas as pl
from jax.experimental.pallas import tpu as pltpu
from jax.sharding import PartitionSpec as P

PG = 4
SIDE = 128
TX = 8
TY = 4
WIN = 32
GROUP = 4
ROWS = SIDE // TY
COLS = SIDE // TX


def basis_table(basis):
    kernels, width = basis.shape[0], basis.shape[1]
    w = np.arange(WIN)[:, None] - np.arange(TX)[None, :]
    wide = jnp.pad(basis.astype(jnp.float32), ((0, 0), (0, 0), (0, 1)), constant_values=0.0)
    index = np.where((w >= 0) & (w < width), w, width)
    hot = (index[None] == np.arange(width)[:, None, None]).astype(np.float32)
    table = jnp.einsum("bij,jwt->iwbt", basis.astype(jnp.bfloat16), jnp.asarray(hot, jnp.bfloat16), preferred_element_type=jnp.float32)
    table = table.reshape(width * WIN, kernels * TX).astype(jnp.bfloat16)
    return jnp.concatenate([table, table], axis=1)


def pick_table(pad):
    p = np.arange(TY)
    x = np.arange(SIDE)
    X = np.arange(COLS)
    w = np.arange(WIN)
    keep = (w < TX + 2 * pad)[None, None, None, None, :]
    hit = (p[:, None, None, None, None] == p[None, None, None, :, None]) & (
        x[None, :, None, None, None] == TX * X[None, None, :, None, None] + w[None, None, None, None, :] - pad) & keep
    return hit.reshape(TY * SIDE, COLS * TY * WIN)


def grids():
    g = (2.0 * np.arange(SIDE) + 1.0 - SIDE) / SIDE
    lane = np.arange(128)
    h, q, t = lane // 32, (lane // 8) % 4, lane % 8
    gx = np.stack([g[8 * (4 * h + lo) + t] for lo in range(4)])
    gy = g[4 * np.arange(ROWS)[:, None] + q[None, :]]
    return np.concatenate([gy, np.pad(gx, ((0, 4), (0, 0)))]).astype(np.float32)


def kernel(width, halves, perm, dest, span, top, bottom, third, shift, *refs):
    coefs, images, taps, ltab, stab, gtab, before, slots = refs[:8]
    spare = refs[8] if halves else None
    squares, wpad, qf, qb, oscr, zscr, held, sems = refs[-8:]
    step = pl.program_id(0)
    first, last = span[0], span[1]
    turn = lax.rem(step, 2)

    def place(s, b):
        return jnp.minimum(first + s * GROUP + b, perm.shape[0] - 1)

    def live(s, b):
        return first + s * GROUP + b < last

    def copies(s, b, act):
        spot, at = lax.rem(s, 2), place(s, b)
        if not halves:
            @pl.when(live(s, b))
            def _():
                act(pltpu.make_async_copy(held.at[spot, b], slots.at[dest[at]], sems.at[spot, b, 0]))
        else:
            @pl.when(jnp.logical_and(live(s, b), third[at] == 0))
            def _():
                for side, slot in enumerate((top[at], bottom[at])):
                    part = held.at[spot, b, pl.ds(side * SIDE // 2, SIDE // 2)]
                    act(pltpu.make_async_copy(part, slots.at[slot], sems.at[spot, b, side]))

            @pl.when(jnp.logical_and(live(s, b), third[at] == 1))
            def _():
                act(pltpu.make_async_copy(held.at[spot, b], spare.at[dest[at]], sems.at[spot, b, 0]))

    def finish(s):
        for b in range(GROUP):
            copies(s, b, lambda one: one.wait())

    halo = width // 2
    groups = (TY + width - 1) // TY
    rlen = 40
    base = 12

    @pl.when(step == 0)
    def _():
        wpad[...] = jnp.zeros_like(wpad)
        squares[...] = before[...]

    @pl.when(jnp.logical_and(step >= 2, first + step * GROUP < last))
    def _():
        finish(step - 2)

    chosen = [perm[place(step, b)] for b in range(GROUP)]
    @pl.when(first + step * GROUP < last)
    def _():
        delta = lax.broadcasted_iota(jnp.int32, (SIDE, SIDE), 0) - lax.broadcasted_iota(jnp.int32, (SIDE, SIDE), 1)
        lane = lax.broadcasted_iota(jnp.int32, (8, 128), 1)

        def band(b, d):
            off = delta - (shift[chosen[b] * 2 + d] - 3)
            total = jnp.zeros((SIDE, SIDE), jnp.float32)
            for k in range(8):
                total = jnp.where(off == k, taps[chosen[b], d, k][None, :], total)
            return total.astype(jnp.bfloat16)

        kernels = ltab.shape[1] // (2 * TX)
        lanes = lax.broadcasted_iota(jnp.int32, (TX, 128), 1)
        same = lax.broadcasted_iota(jnp.int32, (TX, 128), 0) == lanes % TX

        def weights_of(b):
            at = chosen[b] * 3 * kernels
            wide = [jnp.where(same, jnp.where(lanes < 32, coefs[at + i], jnp.where(lanes < 64, coefs[at + kernels + i], coefs[at + 2 * kernels + i])), 0.0) for i in range(kernels)]
            wide = jnp.concatenate(wide, axis=0)
            high = wide.astype(jnp.bfloat16)
            low = (wide - high.astype(jnp.float32)).astype(jnp.bfloat16)
            return jnp.concatenate([high, low], axis=0)

        picked = []
        for b in range(GROUP):
            half = lax.dot_general(band(b, 0), images[chosen[b]], (((0,), (0,)), ((), ())), preferred_element_type=jnp.float32).astype(jnp.bfloat16)
            warped = jnp.dot(half, band(b, 1), preferred_element_type=jnp.float32)
            wpad[b, base:base + SIDE, :] = warped
            phases = [wpad[b, pl.ds(p + base - halo, rlen, stride=TY), :].astype(jnp.bfloat16) for p in range(TY)]
            picked.append(jnp.concatenate(phases, axis=1))
        lhs = jnp.concatenate(picked, axis=0)
        for X in range(0, COLS, 2):
            got = jnp.dot(lhs, stab[:, 128 * X:128 * X + 256], preferred_element_type=jnp.float32)
            for b in range(GROUP):
                for side in range(2):
                    qf[b, pl.ds(X + side, rlen, stride=COLS), :] = got[b * rlen:(b + 1) * rlen, 128 * side:128 * side + 128]
        qsub = (lax.broadcasted_iota(jnp.int32, (WIN, 128), 1) // TX) % TY
        group_of = (lane // 32)[:1]
        sub_of = ((lane // 8) % 4)[:1]

        def choose(which, values):
            result = values[3]
            for i in (2, 1, 0):
                result = jnp.where(which == i, values[i], result)
            return result

        ltable = ltab[...]
        for pair in range(0, GROUP, 2):
            rr = jnp.concatenate([weights_of(pair), weights_of(pair + 1)], axis=1)
            hh = jnp.dot(ltable, rr, preferred_element_type=jnp.float32)
            for b in (pair, pair + 1):
                qb[b] = qf[b].astype(jnp.bfloat16)
                h = hh[:, 128 * (b - pair):128 * (b - pair) + 128]
                zero = jnp.zeros((WIN, 128), jnp.float32)
                parts = []
                for ii in range(width + TY - 1):
                    rows = [h[WIN * (ii - q):WIN * (ii - q) + WIN] if 0 <= ii - q < width else zero for q in range(TY)]
                    parts.append(choose(qsub, rows).astype(jnp.bfloat16))
                weights = jnp.concatenate(parts, axis=0)
                left = jnp.concatenate([qb[b, COLS * g:COLS * g + ROWS * COLS, :] for g in range(groups)], axis=1)
                oscr[b] = jnp.dot(left, weights, preferred_element_type=jnp.float32)
        summed = jnp.zeros((8, 128), jnp.float32)
        for b in range(GROUP):
            mixed = []
            for lo in range(4):
                a = [oscr[b, pl.ds(4 * h + lo, ROWS, stride=COLS), :] for h in range(4)]
                turned = []
                for k in range(4):
                    diag = choose(group_of, [a[(g + k) % 4] for g in range(4)])
                    turned.append(diag if k == 0 else pltpu.roll(diag, 32 * k, 1))
                m = [choose(group_of, [turned[(h - d) % 4] for h in range(4)]) for d in range(3)]
                mixed.append(m[0] + gtab[ROWS + lo:ROWS + lo + 1, :] * m[1] + gtab[:ROWS, :] * m[2])
            turned = []
            for k in range(4):
                diag = choose(sub_of, [mixed[(g + k) % 4] for g in range(4)])
                if k == 0:
                    turned.append(diag)
                else:
                    turned.append(jnp.where(sub_of >= k, pltpu.roll(diag, 8 * k, 1), pltpu.roll(diag, (8 * k - 32) % 128, 1)))
            total = jnp.zeros((8, 128), jnp.float32)
            for q in range(4):
                final = choose(sub_of, [turned[(lo - q) % 4] for lo in range(4)])
                zscr[b, pl.ds(q, ROWS, stride=TY), :] = final
                sq = final * final
                total = total + (sq[0:8] + sq[8:16] + sq[16:24] + sq[24:32])
            held[turn, b] = zscr[b].astype(jnp.bfloat16)
            summed = summed + jnp.where(live(step, b), total, 0.0)

        squares[...] += summed
        for b in range(GROUP):
            copies(step, b, lambda one: one.start())

        if not halves:
            @pl.when(first + (step + 1) * GROUP >= last)
            def _():
                folded = jnp.sum(jnp.sum(squares[...], axis=0, keepdims=True), axis=1, keepdims=True)
                squares[...] = jnp.broadcast_to(folded, (8, 128))

        @pl.when(first + (step + 1) * GROUP >= last)
        def _():
            @pl.when(step >= 1)
            def _():
                finish(step - 1)
            finish(step)


def whole(a):
    return pl.BlockSpec(a.shape, lambda s, *_: (0,) * a.ndim)


def match(lists, halves, most, tables, images, warp_taps, shift, coefs, before, slots):
    count = images.shape[0]
    width = tables[0].shape[0] // WIN
    given = (images, warp_taps, *tables, before)
    sizes = [(slots, SIDE // 2, SIDE), (slots, SIDE, SIDE)] if halves else [(slots, SIDE, SIDE)]
    grid_spec = pltpu.PrefetchScalarGridSpec(
        num_scalar_prefetch=8,
        grid=((most + GROUP - 1) // GROUP,),
        in_specs=[pl.BlockSpec(memory_space=pltpu.VMEM) for _ in given],
        out_specs=[pl.BlockSpec(memory_space=pl.ANY) for _ in sizes] + [
            pl.BlockSpec((8, 128), lambda s, *_: (0, 0)),
        ],
        scratch_shapes=[
            pltpu.VMEM((GROUP, 168, SIDE), jnp.float32),
            pltpu.VMEM((GROUP, 640, 128), jnp.float32),
            pltpu.VMEM((GROUP, 640, 128), jnp.bfloat16),
            pltpu.VMEM((GROUP, 512, 128), jnp.float32),
            pltpu.VMEM((GROUP, 128, 128), jnp.float32),
            pltpu.VMEM((2, GROUP, 128, 128), jnp.bfloat16),
            pltpu.SemaphoreType.DMA((2, GROUP, 2)),
        ],
    )
    return pl.pallas_call(
        functools.partial(kernel, width, halves),
        out_shape=(*[jax.ShapeDtypeStruct(size, jnp.bfloat16) for size in sizes], jax.ShapeDtypeStruct((8, 128), jnp.float32)),
        grid_spec=grid_spec,
        compiler_params=pltpu.CompilerParams(vmem_limit_bytes=62 * 1024 * 1024),
        cost_estimate=pl.CostEstimate(flops=40_000_000_000, bytes_accessed=8_000_000, transcendentals=0),
    )(*lists, shift, coefs, *given)


CHUNK = 16


def gather_sum(labels, scale, step, blocks, total):
    for i in range(CHUNK):
        tile = labels[step * CHUNK + i]

        @pl.when(tile >= 0)
        def _():
            total[tile] += scale[step * CHUNK + i] * blocks[i].astype(jnp.float32)


def spread_out(labels, step, templates, out):
    for i in range(CHUNK):
        tile = labels[step * CHUNK + i]

        @pl.when(tile >= 0)
        def _():
            out[i] = templates[tile]


def partial_kernel(labels, scale, blocks, total):
    step = pl.program_id(0)

    @pl.when(step == 0)
    def _():
        total[...] = jnp.zeros_like(total)

    gather_sum(labels, scale, step, blocks, total)


def coadd_kernel(labels, scale, inverse, blocks, earlier, coadd, templates, out, arrived, total, done, small, leaving, sems):
    parts = arrived.shape[0] // CHUNK
    taken = [pltpu.make_async_copy(earlier, total, sems.at[0])]
    given = [pltpu.make_async_copy(done, coadd, sems.at[1]), pltpu.make_async_copy(small, templates, sems.at[2])]
    for i in range(parts):
        part = pl.ds(i * CHUNK, CHUNK)
        taken.append(pltpu.make_async_copy(blocks.at[part], arrived.at[part], sems.at[3 + i]))
        given.append(pltpu.make_async_copy(leaving.at[part], out.at[part], sems.at[3 + parts + i]))
    for copy in taken:
        copy.start()
    taken[0].wait()
    for i in range(parts):
        taken[1 + i].wait()
        gather_sum(labels, scale, i, arrived.at[pl.ds(i * CHUNK, CHUNK)], total)
    for tile in range(PG * PG):
        value = total[tile] * inverse[tile]
        done[tile] = value
        small[tile] = value.astype(jnp.bfloat16)
    given[0].start()
    given[1].start()
    for i in range(parts):
        spread_out(labels, i, small, leaving.at[pl.ds(i * CHUNK, CHUNK)])
        given[2 + i].start()
    for copy in given:
        copy.wait()


def spread_kernel(labels, templates, out):
    spread_out(labels, pl.program_id(0), templates, out)


def slots_spec(where, height=SIDE):
    return pl.BlockSpec((CHUNK, height, SIDE), lambda s, *_: (where(s), 0, 0))


def partial_sum(labels, scale, blocks, number):
    tiles = (number, blocks.shape[1], SIDE)
    return pl.pallas_call(
        partial_kernel,
        out_shape=jax.ShapeDtypeStruct(tiles, jnp.float32),
        grid_spec=pltpu.PrefetchScalarGridSpec(
            num_scalar_prefetch=2, grid=(blocks.shape[0] // CHUNK,),
            in_specs=[slots_spec(lambda s: s, blocks.shape[1])],
            out_specs=pl.BlockSpec(tiles, lambda s, *_: (0, 0, 0))),
        cost_estimate=pl.CostEstimate(flops=1_000, bytes_accessed=1_000, transcendentals=0),
    )(labels, scale, blocks)


def finish_sum(labels, scale, inverse, blocks, earlier):
    tiles = (PG * PG, SIDE, SIDE)
    anywhere = pl.BlockSpec(memory_space=pl.ANY)
    return pl.pallas_call(
        coadd_kernel,
        out_shape=(jax.ShapeDtypeStruct(tiles, jnp.float32), jax.ShapeDtypeStruct(tiles, jnp.bfloat16), jax.ShapeDtypeStruct(blocks.shape, jnp.bfloat16)),
        grid_spec=pltpu.PrefetchScalarGridSpec(
            num_scalar_prefetch=3, grid=(1,),
            in_specs=[anywhere, anywhere],
            out_specs=[anywhere, anywhere, anywhere],
            scratch_shapes=[
                pltpu.VMEM(blocks.shape, jnp.bfloat16),
                pltpu.VMEM(tiles, jnp.float32),
                pltpu.VMEM(tiles, jnp.float32),
                pltpu.VMEM(tiles, jnp.bfloat16),
                pltpu.VMEM(blocks.shape, jnp.bfloat16),
                pltpu.SemaphoreType.DMA((3 + 2 * (blocks.shape[0] // CHUNK),)),
            ]),
        compiler_params=pltpu.CompilerParams(vmem_limit_bytes=60 * 1024 * 1024),
        cost_estimate=pl.CostEstimate(flops=10_000_000, bytes_accessed=10_000_000, transcendentals=0),
    )(labels, scale, inverse, blocks, earlier)


def spread(labels, templates, slots):
    return pl.pallas_call(
        spread_kernel,
        out_shape=jax.ShapeDtypeStruct((slots,) + templates.shape[1:], jnp.bfloat16),
        grid_spec=pltpu.PrefetchScalarGridSpec(
            num_scalar_prefetch=1, grid=(slots // CHUNK,),
            in_specs=[pl.BlockSpec(templates.shape, lambda s, *_: (0, 0, 0))],
            out_specs=slots_spec(lambda s: s, templates.shape[1])),
        cost_estimate=pl.CostEstimate(flops=10_000_000, bytes_accessed=5_000_000, transcendentals=0),
    )(labels, templates)


def difference_kernel(halves, kind, near, aliased, perm, dest, span, top, bottom, third, sent, template, *refs):
    out, left, right, answer, sems = refs[1:] if aliased else refs
    begin, number = span[0], span[1] - span[0]
    height = sent.shape[1]

    def each(act):
        @pl.loop(0, number)
        def _(i):
            @pl.when(third[begin + i] == kind)
            def _():
                act(i)

    def inward(i):
        for side in range(SIDE // height):
            slot = (top, bottom)[side][begin + i] if halves else dest[begin + i]
            part = pl.ds(side * height, height)
            yield pltpu.make_async_copy(sent.at[slot], left.at[i, part], sems.at[0, side, i])
            if not near:
                yield pltpu.make_async_copy(template.at[slot], right.at[i, part], sems.at[1, side, i])

    def outward(i):
        return pltpu.make_async_copy(answer.at[i], out.at[perm[begin + i]], sems.at[2, 0, i])

    def fetch(i):
        for one in inward(i):
            one.start()

    def work(i):
        for one in inward(i):
            one.wait()
        if near:
            for side, slot in enumerate((top[begin + i], bottom[begin + i])):
                part = pl.ds(side * height, height)
                answer[i, part] = left[i, part].astype(jnp.float32) - template[slot].astype(jnp.float32)
        else:
            answer[i] = left[i].astype(jnp.float32) - right[i].astype(jnp.float32)
        outward(i).start()

    each(fetch)
    each(work)
    each(lambda i: outward(i).wait())


def subtract(lists, halves, kind, most, sent, template, held=None):
    anywhere = pl.BlockSpec(memory_space=pl.ANY)
    more = [] if held is None else [held]
    near = False
    return pl.pallas_call(
        functools.partial(difference_kernel, halves, kind, near, held is not None),
        out_shape=jax.ShapeDtypeStruct((lists[0].shape[0], SIDE, SIDE), jnp.float32),
        grid_spec=pltpu.PrefetchScalarGridSpec(
            num_scalar_prefetch=6, grid=(1,), in_specs=[anywhere, pl.BlockSpec(memory_space=pltpu.VMEM) if near else anywhere] + [anywhere for _ in more], out_specs=anywhere,
            scratch_shapes=[
                pltpu.VMEM((most, SIDE, SIDE), jnp.bfloat16),
                pltpu.VMEM((most, SIDE, SIDE), jnp.bfloat16),
                pltpu.VMEM((most, SIDE, SIDE), jnp.float32),
                pltpu.SemaphoreType.DMA((3, 2, most)),
            ]),
        input_output_aliases={8: 0} if more else {},
        compiler_params=pltpu.CompilerParams(vmem_limit_bytes=62 * 1024 * 1024),
        cost_estimate=pl.CostEstimate(flops=1_000_000, bytes_accessed=2_000_000, transcendentals=0),
    )(*lists, sent, template, *more)


def nothing(out):
    pass


def unused(like):
    return pl.pallas_call(
        nothing,
        out_shape=jax.ShapeDtypeStruct(like.shape, like.dtype),
        out_specs=pl.BlockSpec(memory_space=pl.ANY),
    )()


def body(images, warp_taps, warp_shift, psf_coefs, psf_basis, owner, offsets):
    axes = ("visit", "det")
    count = images.shape[0]
    n_visit, n_det = (lax.axis_size("visit"), lax.axis_size("det"))
    devices = n_visit * n_det
    target = owner[:, 0]
    tile = offsets[:, 0] * PG + offsets[:, 1]
    order = jnp.arange(count, dtype=jnp.int32)
    second = jnp.any((target[:, None] == target[None, :]) & (order[:, None] > order[None, :]), axis=1)
    seconds = jnp.sum(second.astype(jnp.int32))
    before_me = order[None, :] < order[:, None]
    lower = jnp.sum((before_me & (second[None, :] == second[:, None])).astype(jnp.int32), axis=1)
    position = jnp.where(second, lower, seconds + lower)
    put = position[None, :] == order[:, None]
    def partner(device, way):
        visit, det = device // n_det, device % n_det
        return (visit + 1 - 2 * (visit % 2)) * n_det + det if way == 0 else device + 1 - 2 * (det % 2)

    def half_of(device):
        return (device // n_det + device % n_det) % 2

    def clashes(way):
        pair = jnp.minimum(target, partner(target, way))
        return second & jnp.any(second[None, :] & (pair[:, None] == pair[None, :]) & before_me, axis=1)

    clash = [clashes(way) for way in range(2)]
    other_way = jnp.any(clash[0]) & ~jnp.any(clash[1])
    extra = jnp.where(other_way, clash[1], clash[0])
    mate = jnp.where(other_way, partner(target, 1), partner(target, 0))
    lower = half_of(target) == 1
    packed = ((lower.astype(jnp.int32) * 2 + extra.astype(jnp.int32)) * devices + mate) * devices + target
    packed = jnp.sum(jnp.where(put, (packed * count + order)[None, :], 0), axis=1)
    perm, dest, mates = packed % count, packed // count % devices, packed // (count * devices) % devices
    flags = packed // (count * devices * devices)
    third = flags % 2
    top, bottom = jnp.where(flags >= 2, mates, dest), jnp.where(flags >= 2, dest, mates)
    zero = jnp.zeros((), jnp.int32)
    span_second = jnp.stack([zero, seconds])
    span_first = jnp.stack([seconds, zero + count])
    lists = lambda span: (perm, dest, span, top, bottom, third)

    tables = (basis_table(psf_basis), jnp.asarray(pick_table(psf_basis.shape[1] // 2), jnp.bfloat16), jnp.asarray(grids()))
    ours = (images, warp_taps, warp_shift.reshape(-1), psf_coefs.reshape(-1))
    exchange = lambda a: lax.all_to_all(a, axes, split_axis=0, concat_axis=0, tiled=True)
    out_second, out_third, squares = match(lists(span_second), True, count // 2, tables, *ours, jnp.zeros((8, 128), jnp.float32), devices)
    in_second = exchange(out_second)
    out_first, squares = match(lists(span_first), False, count, tables, *ours, squares, devices)
    everyone = jnp.arange(devices, dtype=jnp.int32)[:, None]
    label = lambda named, what: jnp.max(jnp.where(named, what, -1), axis=1).astype(jnp.float32)
    here = target[None, :] == everyone
    near = mate[None, :] == everyone
    tiles = PG * PG
    note = jnp.stack([
        label(here & ~second[None, :], tile[None, :]),
        label((here | near) & (second & ~extra)[None, :], tile[None, :] + jnp.where(here, 0, jnp.where(other_way, 2 * tiles, tiles))),
        label(here & extra[None, :], tile[None, :]),
        jnp.full((devices,), jnp.max(extra.astype(jnp.float32))),
        jnp.full((devices,), other_way.astype(jnp.float32)),
        jnp.full((devices,), squares[0, 0])], axis=1)
    in_second, out_first, note = lax.optimization_barrier((in_second, out_first, note))
    notes = exchange(note)
    some_third, some_other = jnp.max(notes[:, 3]) > 0, jnp.max(notes[:, 4]) > 0
    in_third = lax.cond(some_third, exchange, unused, out_third)
    in_third, out_first = lax.optimization_barrier((in_third, out_first))
    in_first = exchange(out_first)
    power = notes[:, 5].reshape(n_visit, n_det).sum(axis=1)
    entries = count * SIDE * SIDE * n_det
    weight = lax.reduce_precision(1.0 / (power / entries + 1e-06), 8, 7)
    scale = jnp.repeat(weight, n_det)
    label_first, label_second, label_third = [notes[:, i].astype(jnp.int32) for i in range(3)]

    upper = (lax.axis_index("visit") + lax.axis_index("det")) % 2 == 1
    to_first = lambda a: lax.ppermute(a, "visit", [(v, v ^ 1) for v in range(n_visit)])
    to_second = lambda a: lax.cond(some_other, lambda b: lax.ppermute(b, "det", [(d, d ^ 1) for d in range(n_det)]), lambda b: b, a)
    parts = partial_sum(label_second, scale, in_second, 3 * tiles)
    own = parts[:tiles]
    their = to_first(parts[tiles:2 * tiles]) + to_second(parts[2 * tiles:])
    earlier = jnp.concatenate([jnp.where(upper, their, own), jnp.where(upper, own, their)], axis=1)
    earlier = earlier + partial_sum(label_third, scale, in_third, tiles)
    kinds = jnp.arange(tiles, dtype=jnp.int32)[:, None]
    hits = sum((a[None] == kinds).astype(jnp.float32) for a in (label_first, label_second, label_third))
    inverse = 1.0 / jnp.maximum(jnp.sum(hits * scale[None], axis=1), 0.25)

    coadd, templates, back_first = finish_sum(label_first, scale, inverse, in_first, earlier)
    home_third = lax.cond(some_third, lambda a: exchange(spread(label_third, a, devices)), lambda a: unused(out_third), templates)
    home_third, back_first = lax.optimization_barrier((home_third, back_first))
    home_first = exchange(back_first)
    above, below = templates[:, :SIDE // 2], templates[:, SIDE // 2:]
    across = jnp.where(upper, above, below)
    both = jnp.concatenate([jnp.where(upper, below, above)] + [to_first(across), to_second(across)], axis=0)
    home_second = exchange(spread(label_second, both, devices))
    difference = subtract(lists(span_first), 0, 0, count, out_first, home_first)
    difference = subtract(lists(span_second), 0, 1, count // 2, out_third, home_third, difference)
    difference = subtract(lists(span_second), 1, 0, count // 2, out_second, home_second, difference)
    return (difference, coadd)


def solution(mesh):
    in_specs = (
        P(("visit", "det"), None, None),
        P(("visit", "det"), None, None, None),
        P(("visit", "det"), None),
        P(("visit", "det"), None, None),
        P(),
        P(("visit", "det"), None),
        P(("visit", "det"), None),
    )
    out_specs = (P(("visit", "det"), None, None), P(("visit", "det"), None, None))
    return jax.shard_map(body, mesh=mesh, in_specs=in_specs, out_specs=out_specs, check_vma=False)
```

```python
import functools

import jax
import jax.numpy as jnp
import numpy as np
from jax import lax
from jax.experimental import pallas as pl
from jax.experimental.pallas import tpu as pltpu
from jax.sharding import PartitionSpec as P

PG = 4
SIDE = 128
TX = 8
TY = 4
WIN = 32
GROUP = 8
ROWS = SIDE // TY
COLS = SIDE // TX


def basis_table(basis):
    kernels, width = basis.shape[0], basis.shape[1]
    w = np.arange(WIN)[:, None] - np.arange(TX)[None, :]
    wide = jnp.pad(basis.astype(jnp.float32), ((0, 0), (0, 0), (0, 1)), constant_values=0.0)
    index = np.where((w >= 0) & (w < width), w, width)
    hot = (index[None] == np.arange(width)[:, None, None]).astype(np.float32)
    table = jnp.einsum("bij,jwt->iwbt", basis.astype(jnp.bfloat16), jnp.asarray(hot, jnp.bfloat16), preferred_element_type=jnp.float32)
    table = table.reshape(width * WIN, kernels * TX).astype(jnp.bfloat16)
    return jnp.concatenate([table, table], axis=1)


def pick_table(pad):
    p = np.arange(TY)
    x = np.arange(SIDE)
    X = np.arange(COLS)
    w = np.arange(WIN)
    keep = (w < TX + 2 * pad)[None, None, None, None, :]
    hit = (p[:, None, None, None, None] == p[None, None, None, :, None]) & (
        x[None, :, None, None, None] == TX * X[None, None, :, None, None] + w[None, None, None, None, :] - pad) & keep
    return hit.reshape(TY * SIDE, COLS * TY * WIN)


def grids():
    g = (2.0 * np.arange(SIDE) + 1.0 - SIDE) / SIDE
    lane = np.arange(128)
    h, q, t = lane // 32, (lane // 8) % 4, lane % 8
    gx = np.stack([g[8 * (4 * h + lo) + t] for lo in range(4)])
    gy = g[4 * np.arange(ROWS)[:, None] + q[None, :]]
    return np.concatenate([gy, np.pad(gx, ((0, 4), (0, 0)))]).astype(np.float32)


def kernel(width, halves, perm, dest, span, top, bottom, third, shift, *refs):
    coefs, images, taps, ltab, stab, gtab, before, slots = refs[:8]
    spare = refs[8] if halves else None
    squares, wpad, qf, qb, oscr, zscr, held, sems = refs[-8:]
    step = pl.program_id(0)
    first, last = span[0], span[1]
    turn = lax.rem(step, 2)

    def place(s, b):
        return jnp.minimum(first + s * GROUP + b, perm.shape[0] - 1)

    def live(s, b):
        return first + s * GROUP + b < last

    def copies(s, b, act):
        spot, at = lax.rem(s, 2), place(s, b)
        if not halves:
            @pl.when(live(s, b))
            def _():
                act(pltpu.make_async_copy(held.at[spot, b], slots.at[dest[at]], sems.at[spot, b, 0]))
        else:
            @pl.when(jnp.logical_and(live(s, b), third[at] == 0))
            def _():
                for side, slot in enumerate((top[at], bottom[at])):
                    part = held.at[spot, b, pl.ds(side * SIDE // 2, SIDE // 2)]
                    act(pltpu.make_async_copy(part, slots.at[slot], sems.at[spot, b, side]))

            @pl.when(jnp.logical_and(live(s, b), third[at] == 1))
            def _():
                act(pltpu.make_async_copy(held.at[spot, b], spare.at[dest[at]], sems.at[spot, b, 0]))

    def finish(s):
        for b in range(GROUP):
            copies(s, b, lambda one: one.wait())

    halo = width // 2
    groups = (TY + width - 1) // TY
    rlen = 40
    base = 12

    @pl.when(step == 0)
    def _():
        wpad[...] = jnp.zeros_like(wpad)
        squares[...] = before[...]

    @pl.when(jnp.logical_and(step >= 2, first + step * GROUP < last))
    def _():
        finish(step - 2)

    chosen = [perm[place(step, b)] for b in range(GROUP)]
    @pl.when(first + step * GROUP < last)
    def _():
        delta = lax.broadcasted_iota(jnp.int32, (SIDE, SIDE), 0) - lax.broadcasted_iota(jnp.int32, (SIDE, SIDE), 1)
        lane = lax.broadcasted_iota(jnp.int32, (8, 128), 1)

        def band(b, d):
            off = delta - (shift[chosen[b] * 2 + d] - 3)
            total = jnp.zeros((SIDE, SIDE), jnp.float32)
            for k in range(8):
                total = jnp.where(off == k, taps[chosen[b], d, k][None, :], total)
            return total.astype(jnp.bfloat16)

        kernels = ltab.shape[1] // (2 * TX)
        lanes = lax.broadcasted_iota(jnp.int32, (TX, 128), 1)
        same = lax.broadcasted_iota(jnp.int32, (TX, 128), 0) == lanes % TX

        def weights_of(b):
            at = chosen[b] * 3 * kernels
            wide = [jnp.where(same, jnp.where(lanes < 32, coefs[at + i], jnp.where(lanes < 64, coefs[at + kernels + i], coefs[at + 2 * kernels + i])), 0.0) for i in range(kernels)]
            wide = jnp.concatenate(wide, axis=0)
            high = wide.astype(jnp.bfloat16)
            low = (wide - high.astype(jnp.float32)).astype(jnp.bfloat16)
            return jnp.concatenate([high, low], axis=0)

        picked = []
        for b in range(GROUP):
            half = lax.dot_general(band(b, 0), images[chosen[b]], (((0,), (0,)), ((), ())), preferred_element_type=jnp.float32).astype(jnp.bfloat16)
            warped = jnp.dot(half, band(b, 1), preferred_element_type=jnp.float32)
            wpad[b, base:base + SIDE, :] = warped
            phases = [wpad[b, pl.ds(p + base - halo, rlen, stride=TY), :].astype(jnp.bfloat16) for p in range(TY)]
            picked.append(jnp.concatenate(phases, axis=1))
        lhs = jnp.concatenate(picked, axis=0)
        for X in range(0, COLS, 2):
            got = jnp.dot(lhs, stab[:, 128 * X:128 * X + 256], preferred_element_type=jnp.float32)
            for b in range(GROUP):
                for side in range(2):
                    qf[b, pl.ds(X + side, rlen, stride=COLS), :] = got[b * rlen:(b + 1) * rlen, 128 * side:128 * side + 128]
        qsub = (lax.broadcasted_iota(jnp.int32, (WIN, 128), 1) // TX) % TY
        group_of = (lane // 32)[:1]
        sub_of = ((lane // 8) % 4)[:1]

        def choose(which, values):
            result = values[3]
            for i in (2, 1, 0):
                result = jnp.where(which == i, values[i], result)
            return result

        ltable = ltab[...]
        for pair in range(0, GROUP, 2):
            rr = jnp.concatenate([weights_of(pair), weights_of(pair + 1)], axis=1)
            hh = jnp.dot(ltable, rr, preferred_element_type=jnp.float32)
            for b in (pair, pair + 1):
                qb[b] = qf[b].astype(jnp.bfloat16)
                h = hh[:, 128 * (b - pair):128 * (b - pair) + 128]
                zero = jnp.zeros((WIN, 128), jnp.float32)
                parts = []
                for ii in range(width + TY - 1):
                    rows = [h[WIN * (ii - q):WIN * (ii - q) + WIN] if 0 <= ii - q < width else zero for q in range(TY)]
                    parts.append(choose(qsub, rows).astype(jnp.bfloat16))
                weights = jnp.concatenate(parts, axis=0)
                left = jnp.concatenate([qb[b, COLS * g:COLS * g + ROWS * COLS, :] for g in range(groups)], axis=1)
                oscr[b] = jnp.dot(left, weights, preferred_element_type=jnp.float32)
        summed = jnp.zeros((8, 128), jnp.float32)
        for b in range(GROUP):
            mixed = []
            for lo in range(4):
                a = [oscr[b, pl.ds(4 * h + lo, ROWS, stride=COLS), :] for h in range(4)]
                turned = []
                for k in range(4):
                    diag = choose(group_of, [a[(g + k) % 4] for g in range(4)])
                    turned.append(diag if k == 0 else pltpu.roll(diag, 32 * k, 1))
                m = [choose(group_of, [turned[(h - d) % 4] for h in range(4)]) for d in range(3)]
                mixed.append(m[0] + gtab[ROWS + lo:ROWS + lo + 1, :] * m[1] + gtab[:ROWS, :] * m[2])
            turned = []
            for k in range(4):
                diag = choose(sub_of, [mixed[(g + k) % 4] for g in range(4)])
                if k == 0:
                    turned.append(diag)
                else:
                    turned.append(jnp.where(sub_of >= k, pltpu.roll(diag, 8 * k, 1), pltpu.roll(diag, (8 * k - 32) % 128, 1)))
            total = jnp.zeros((8, 128), jnp.float32)
            for q in range(4):
                final = choose(sub_of, [turned[(lo - q) % 4] for lo in range(4)])
                zscr[b, pl.ds(q, ROWS, stride=TY), :] = final
                sq = final * final
                total = total + (sq[0:8] + sq[8:16] + sq[16:24] + sq[24:32])
            held[turn, b] = zscr[b].astype(jnp.bfloat16)
            summed = summed + jnp.where(live(step, b), total, 0.0)

        squares[...] += summed
        for b in range(GROUP):
            copies(step, b, lambda one: one.start())

        if not halves:
            @pl.when(first + (step + 1) * GROUP >= last)
            def _():
                folded = jnp.sum(jnp.sum(squares[...], axis=0, keepdims=True), axis=1, keepdims=True)
                squares[...] = jnp.broadcast_to(folded, (8, 128))

        @pl.when(first + (step + 1) * GROUP >= last)
        def _():
            @pl.when(step >= 1)
            def _():
                finish(step - 1)
            finish(step)


def whole(a):
    return pl.BlockSpec(a.shape, lambda s, *_: (0,) * a.ndim)


def match(lists, halves, most, tables, images, warp_taps, shift, coefs, before, slots):
    count = images.shape[0]
    width = tables[0].shape[0] // WIN
    given = (images, warp_taps, *tables, before)
    sizes = [(slots, SIDE // 2, SIDE), (slots, SIDE, SIDE)] if halves else [(slots, SIDE, SIDE)]
    grid_spec = pltpu.PrefetchScalarGridSpec(
        num_scalar_prefetch=8,
        grid=((most + GROUP - 1) // GROUP,),
        in_specs=[pl.BlockSpec(memory_space=pltpu.VMEM) for _ in given],
        out_specs=[pl.BlockSpec(memory_space=pl.ANY) for _ in sizes] + [
            pl.BlockSpec((8, 128), lambda s, *_: (0, 0)),
        ],
        scratch_shapes=[
            pltpu.VMEM((GROUP, 168, SIDE), jnp.float32),
            pltpu.VMEM((GROUP, 640, 128), jnp.float32),
            pltpu.VMEM((GROUP, 640, 128), jnp.bfloat16),
            pltpu.VMEM((GROUP, 512, 128), jnp.float32),
            pltpu.VMEM((GROUP, 128, 128), jnp.float32),
            pltpu.VMEM((2, GROUP, 128, 128), jnp.bfloat16),
            pltpu.SemaphoreType.DMA((2, GROUP, 2)),
        ],
    )
    return pl.pallas_call(
        functools.partial(kernel, width, halves),
        out_shape=(*[jax.ShapeDtypeStruct(size, jnp.bfloat16) for size in sizes], jax.ShapeDtypeStruct((8, 128), jnp.float32)),
        grid_spec=grid_spec,
        compiler_params=pltpu.CompilerParams(vmem_limit_bytes=62 * 1024 * 1024),
        cost_estimate=pl.CostEstimate(flops=40_000_000_000, bytes_accessed=8_000_000, transcendentals=0),
    )(*lists, shift, coefs, *given)


CHUNK = 16


def gather_sum(labels, scale, step, blocks, total):
    for i in range(CHUNK):
        tile = labels[step * CHUNK + i]

        @pl.when(tile >= 0)
        def _():
            total[tile] += scale[step * CHUNK + i] * blocks[i].astype(jnp.float32)


def spread_out(labels, step, templates, out):
    for i in range(CHUNK):
        tile = labels[step * CHUNK + i]

        @pl.when(tile >= 0)
        def _():
            out[i] = templates[tile]


def partial_kernel(labels, scale, blocks, total):
    step = pl.program_id(0)

    @pl.when(step == 0)
    def _():
        total[...] = jnp.zeros_like(total)

    gather_sum(labels, scale, step, blocks, total)


def coadd_kernel(labels, scale, inverse, blocks, earlier, coadd, templates, out, arrived, total, done, small, leaving, sems):
    parts = arrived.shape[0] // CHUNK
    taken = [pltpu.make_async_copy(earlier, total, sems.at[0])]
    given = [pltpu.make_async_copy(done, coadd, sems.at[1]), pltpu.make_async_copy(small, templates, sems.at[2])]
    for i in range(parts):
        part = pl.ds(i * CHUNK, CHUNK)
        taken.append(pltpu.make_async_copy(blocks.at[part], arrived.at[part], sems.at[3 + i]))
        given.append(pltpu.make_async_copy(leaving.at[part], out.at[part], sems.at[3 + parts + i]))
    for copy in taken:
        copy.start()
    taken[0].wait()
    for i in range(parts):
        taken[1 + i].wait()
        gather_sum(labels, scale, i, arrived.at[pl.ds(i * CHUNK, CHUNK)], total)
    for tile in range(PG * PG):
        value = total[tile] * inverse[tile]
        done[tile] = value
        small[tile] = value.astype(jnp.bfloat16)
    given[0].start()
    given[1].start()
    for i in range(parts):
        spread_out(labels, i, small, leaving.at[pl.ds(i * CHUNK, CHUNK)])
        given[2 + i].start()
    for copy in given:
        copy.wait()


def spread_kernel(labels, templates, out):
    spread_out(labels, pl.program_id(0), templates, out)


def slots_spec(where, height=SIDE):
    return pl.BlockSpec((CHUNK, height, SIDE), lambda s, *_: (where(s), 0, 0))


def partial_sum(labels, scale, blocks, number):
    tiles = (number, blocks.shape[1], SIDE)
    return pl.pallas_call(
        partial_kernel,
        out_shape=jax.ShapeDtypeStruct(tiles, jnp.float32),
        grid_spec=pltpu.PrefetchScalarGridSpec(
            num_scalar_prefetch=2, grid=(blocks.shape[0] // CHUNK,),
            in_specs=[slots_spec(lambda s: s, blocks.shape[1])],
            out_specs=pl.BlockSpec(tiles, lambda s, *_: (0, 0, 0))),
        cost_estimate=pl.CostEstimate(flops=1_000, bytes_accessed=1_000, transcendentals=0),
    )(labels, scale, blocks)


def finish_sum(labels, scale, inverse, blocks, earlier):
    tiles = (PG * PG, SIDE, SIDE)
    anywhere = pl.BlockSpec(memory_space=pl.ANY)
    return pl.pallas_call(
        coadd_kernel,
        out_shape=(jax.ShapeDtypeStruct(tiles, jnp.float32), jax.ShapeDtypeStruct(tiles, jnp.bfloat16), jax.ShapeDtypeStruct(blocks.shape, jnp.bfloat16)),
        grid_spec=pltpu.PrefetchScalarGridSpec(
            num_scalar_prefetch=3, grid=(1,),
            in_specs=[anywhere, anywhere],
            out_specs=[anywhere, anywhere, anywhere],
            scratch_shapes=[
                pltpu.VMEM(blocks.shape, jnp.bfloat16),
                pltpu.VMEM(tiles, jnp.float32),
                pltpu.VMEM(tiles, jnp.float32),
                pltpu.VMEM(tiles, jnp.bfloat16),
                pltpu.VMEM(blocks.shape, jnp.bfloat16),
                pltpu.SemaphoreType.DMA((3 + 2 * (blocks.shape[0] // CHUNK),)),
            ]),
        compiler_params=pltpu.CompilerParams(vmem_limit_bytes=60 * 1024 * 1024),
        cost_estimate=pl.CostEstimate(flops=10_000_000, bytes_accessed=10_000_000, transcendentals=0),
    )(labels, scale, inverse, blocks, earlier)


def spread(labels, templates, slots):
    return pl.pallas_call(
        spread_kernel,
        out_shape=jax.ShapeDtypeStruct((slots,) + templates.shape[1:], jnp.bfloat16),
        grid_spec=pltpu.PrefetchScalarGridSpec(
            num_scalar_prefetch=1, grid=(slots // CHUNK,),
            in_specs=[pl.BlockSpec(templates.shape, lambda s, *_: (0, 0, 0))],
            out_specs=slots_spec(lambda s: s, templates.shape[1])),
        cost_estimate=pl.CostEstimate(flops=10_000_000, bytes_accessed=5_000_000, transcendentals=0),
    )(labels, templates)


def difference_kernel(halves, kind, near, aliased, perm, dest, span, top, bottom, third, sent, template, *refs):
    out, left, right, answer, sems = refs[1:] if aliased else refs
    begin, number = span[0], span[1] - span[0]
    height = sent.shape[1]

    def each(act):
        @pl.loop(0, number)
        def _(i):
            @pl.when(third[begin + i] == kind)
            def _():
                act(i)

    def inward(i):
        for side in range(SIDE // height):
            slot = (top, bottom)[side][begin + i] if halves else dest[begin + i]
            part = pl.ds(side * height, height)
            yield pltpu.make_async_copy(sent.at[slot], left.at[i, part], sems.at[0, side, i])
            if not near:
                yield pltpu.make_async_copy(template.at[slot], right.at[i, part], sems.at[1, side, i])

    def outward(i):
        return pltpu.make_async_copy(answer.at[i], out.at[perm[begin + i]], sems.at[2, 0, i])

    def fetch(i):
        for one in inward(i):
            one.start()

    def work(i):
        for one in inward(i):
            one.wait()
        if near:
            for side, slot in enumerate((top[begin + i], bottom[begin + i])):
                part = pl.ds(side * height, height)
                answer[i, part] = left[i, part].astype(jnp.float32) - template[slot].astype(jnp.float32)
        else:
            answer[i] = left[i].astype(jnp.float32) - right[i].astype(jnp.float32)
        outward(i).start()

    each(fetch)
    each(work)
    each(lambda i: outward(i).wait())


def subtract(lists, halves, kind, most, sent, template, held=None):
    anywhere = pl.BlockSpec(memory_space=pl.ANY)
    more = [] if held is None else [held]
    near = False
    return pl.pallas_call(
        functools.partial(difference_kernel, halves, kind, near, held is not None),
        out_shape=jax.ShapeDtypeStruct((lists[0].shape[0], SIDE, SIDE), jnp.float32),
        grid_spec=pltpu.PrefetchScalarGridSpec(
            num_scalar_prefetch=6, grid=(1,), in_specs=[anywhere, pl.BlockSpec(memory_space=pltpu.VMEM) if near else anywhere] + [anywhere for _ in more], out_specs=anywhere,
            scratch_shapes=[
                pltpu.VMEM((most, SIDE, SIDE), jnp.bfloat16),
                pltpu.VMEM((most, SIDE, SIDE), jnp.bfloat16),
                pltpu.VMEM((most, SIDE, SIDE), jnp.float32),
                pltpu.SemaphoreType.DMA((3, 2, most)),
            ]),
        input_output_aliases={8: 0} if more else {},
        compiler_params=pltpu.CompilerParams(vmem_limit_bytes=62 * 1024 * 1024),
        cost_estimate=pl.CostEstimate(flops=1_000_000, bytes_accessed=2_000_000, transcendentals=0),
    )(*lists, sent, template, *more)


def nothing(out):
    pass


def unused(like):
    return pl.pallas_call(
        nothing,
        out_shape=jax.ShapeDtypeStruct(like.shape, like.dtype),
        out_specs=pl.BlockSpec(memory_space=pl.ANY),
    )()


def body(images, warp_taps, warp_shift, psf_coefs, psf_basis, owner, offsets):
    axes = ("visit", "det")
    count = images.shape[0]
    n_visit, n_det = (lax.axis_size("visit"), lax.axis_size("det"))
    devices = n_visit * n_det
    target = owner[:, 0]
    tile = offsets[:, 0] * PG + offsets[:, 1]
    order = jnp.arange(count, dtype=jnp.int32)
    second = jnp.any((target[:, None] == target[None, :]) & (order[:, None] > order[None, :]), axis=1)
    seconds = jnp.sum(second.astype(jnp.int32))
    before_me = order[None, :] < order[:, None]
    lower = jnp.sum((before_me & (second[None, :] == second[:, None])).astype(jnp.int32), axis=1)
    position = jnp.where(second, lower, seconds + lower)
    put = position[None, :] == order[:, None]
    def partner(device, way):
        visit, det = device // n_det, device % n_det
        return (visit + 1 - 2 * (visit % 2)) * n_det + det if way == 0 else device + 1 - 2 * (det % 2)

    def half_of(device):
        return (device // n_det + device % n_det) % 2

    def clashes(way):
        pair = jnp.minimum(target, partner(target, way))
        return second & jnp.any(second[None, :] & (pair[:, None] == pair[None, :]) & before_me, axis=1)

    clash = [clashes(way) for way in range(2)]
    other_way = jnp.any(clash[0]) & ~jnp.any(clash[1])
    extra = jnp.where(other_way, clash[1], clash[0])
    mate = jnp.where(other_way, partner(target, 1), partner(target, 0))
    lower = half_of(target) == 1
    packed = ((lower.astype(jnp.int32) * 2 + extra.astype(jnp.int32)) * devices + mate) * devices + target
    packed = jnp.sum(jnp.where(put, (packed * count + order)[None, :], 0), axis=1)
    perm, dest, mates = packed % count, packed // count % devices, packed // (count * devices) % devices
    flags = packed // (count * devices * devices)
    third = flags % 2
    top, bottom = jnp.where(flags >= 2, mates, dest), jnp.where(flags >= 2, dest, mates)
    zero = jnp.zeros((), jnp.int32)
    span_second = jnp.stack([zero, seconds])
    span_first = jnp.stack([seconds, zero + count])
    lists = lambda span: (perm, dest, span, top, bottom, third)

    tables = (basis_table(psf_basis), jnp.asarray(pick_table(psf_basis.shape[1] // 2), jnp.bfloat16), jnp.asarray(grids()))
    ours = (images, warp_taps, warp_shift.reshape(-1), psf_coefs.reshape(-1))
    exchange = lambda a: lax.all_to_all(a, axes, split_axis=0, concat_axis=0, tiled=True)
    out_second, out_third, squares = match(lists(span_second), True, count // 2, tables, *ours, jnp.zeros((8, 128), jnp.float32), devices)
    in_second = exchange(out_second)
    out_first, squares = match(lists(span_first), False, count, tables, *ours, squares, devices)
    everyone = jnp.arange(devices, dtype=jnp.int32)[:, None]
    label = lambda named, what: jnp.max(jnp.where(named, what, -1), axis=1).astype(jnp.float32)
    here = target[None, :] == everyone
    near = mate[None, :] == everyone
    tiles = PG * PG
    note = jnp.stack([
        label(here & ~second[None, :], tile[None, :]),
        label((here | near) & (second & ~extra)[None, :], tile[None, :] + jnp.where(here, 0, jnp.where(other_way, 2 * tiles, tiles))),
        label(here & extra[None, :], tile[None, :]),
        jnp.full((devices,), jnp.max(extra.astype(jnp.float32))),
        jnp.full((devices,), other_way.astype(jnp.float32)),
        jnp.full((devices,), squares[0, 0])], axis=1)
    in_second, out_first, note = lax.optimization_barrier((in_second, out_first, note))
    notes = exchange(note)
    some_third, some_other = jnp.max(notes[:, 3]) > 0, jnp.max(notes[:, 4]) > 0
    in_third = lax.cond(some_third, exchange, unused, out_third)
    in_third, out_first = lax.optimization_barrier((in_third, out_first))
    in_first = exchange(out_first)
    power = notes[:, 5].reshape(n_visit, n_det).sum(axis=1)
    entries = count * SIDE * SIDE * n_det
    weight = lax.reduce_precision(1.0 / (power / entries + 1e-06), 8, 7)
    scale = jnp.repeat(weight, n_det)
    label_first, label_second, label_third = [notes[:, i].astype(jnp.int32) for i in range(3)]

    upper = (lax.axis_index("visit") + lax.axis_index("det")) % 2 == 1
    to_first = lambda a: lax.ppermute(a, "visit", [(v, v ^ 1) for v in range(n_visit)])
    to_second = lambda a: lax.cond(some_other, lambda b: lax.ppermute(b, "det", [(d, d ^ 1) for d in range(n_det)]), lambda b: b, a)
    parts = partial_sum(label_second, scale, in_second, 3 * tiles)
    own = parts[:tiles]
    their = to_first(parts[tiles:2 * tiles]) + to_second(parts[2 * tiles:])
    earlier = jnp.concatenate([jnp.where(upper, their, own), jnp.where(upper, own, their)], axis=1)
    earlier = earlier + partial_sum(label_third, scale, in_third, tiles)
    kinds = jnp.arange(tiles, dtype=jnp.int32)[:, None]
    hits = sum((a[None] == kinds).astype(jnp.float32) for a in (label_first, label_second, label_third))
    inverse = 1.0 / jnp.maximum(jnp.sum(hits * scale[None], axis=1), 0.25)

    coadd, templates, back_first = finish_sum(label_first, scale, inverse, in_first, earlier)
    home_third = lax.cond(some_third, lambda a: exchange(spread(label_third, a, devices)), lambda a: unused(out_third), templates)
    home_third, back_first = lax.optimization_barrier((home_third, back_first))
    home_first = exchange(back_first)
    above, below = templates[:, :SIDE // 2], templates[:, SIDE // 2:]
    across = jnp.where(upper, above, below)
    both = jnp.concatenate([jnp.where(upper, below, above)] + [to_first(across), to_second(across)], axis=0)
    home_second = exchange(spread(label_second, both, devices))
    difference = subtract(lists(span_first), 0, 0, count, out_first, home_first)
    difference = subtract(lists(span_second), 0, 1, count // 2, out_third, home_third, difference)
    difference = subtract(lists(span_second), 1, 0, count // 2, out_second, home_second, difference)
    return (difference, coadd)


def solution(mesh):
    in_specs = (
        P(("visit", "det"), None, None),
        P(("visit", "det"), None, None, None),
        P(("visit", "det"), None),
        P(("visit", "det"), None, None),
        P(),
        P(("visit", "det"), None),
        P(("visit", "det"), None),
    )
    out_specs = (P(("visit", "det"), None, None), P(("visit", "det"), None, None))
    return jax.shard_map(body, mesh=mesh, in_specs=in_specs, out_specs=out_specs, check_vma=False)
```
